32 devices in a mesh: visit: 8 (over y, x, core), ccd: 4 (over z).
Axes of the slice: x: 2, y: 2, z: 4, core: 2. Of those that a mesh axis runs over, the one named last changes fastest.
Arguments:
- raw_rows: bfloat16 [32, 4096, 128], P('visit', 'ccd')
- resample: bfloat16 [32, 128, 128], P('visit')
- slot_row: int32 [8, 4, 8, 128], P('visit', 'ccd'), may hold values from 0 to 4092, as said below
- tap_weight: float32 [4, 8, 4, 8, 128], P(None, 'visit', 'ccd'), may hold values from 0 to 1
- patch_id: int32 [8, 4, 8, 128], P('visit', 'ccd'), may hold values from 0 to 15
- live_mask: int32 [8, 4, 8, 128], P('visit', 'ccd'), may hold values 0 or 1
Outputs:
- offsets: float32 [32, 64], P('visit')
- background: float32 [512, 128], P(('visit', 'ccd'))
The draws below stay inside these ranges and needn't reach their ends.
Inputs may be any that keep to these rules, and one draw needn't show every extreme that they name: `slot_row`: each value is v * 1024 + b with v below 4 and b at most 1020.
All inputs are finite; a program needn't handle non-finite values. No bound on the sum of `live_mask` on one device may be relied on, other than what follows from the above.
Results may differ from the reference program's by a relative error of at most 0.0041.
Values may be sent and summed in bfloat16 or wider, within the bound.
A program may use at most 64 MiB of HBM per device.

```python
import math
import jax
import jax.numpy as jnp
import numpy as np
from jax import lax

PIX = 128
ORDER = 8
TAPS = 4
ITERS = 2
VIS_DEV = 4
R_DEV = 1024
SLOT = 128
P_DEV = 16
NTERM = 64
VISITS = 32
ROWS_VIS = 4096
PATCHES = 512
N_VISIT = 8
N_CCD = 4


def draw_raw_rows(key, part):
    noise_key, level_key = jax.random.split(key)
    levels = jax.random.normal(level_key, (VISITS, 4), jnp.float32)
    coord_y = (2 * jnp.arange(ROWS_VIS) + 1).astype(jnp.float32) / ROWS_VIS - 1.0
    coord_x = (2 * jnp.arange(PIX) + 1).astype(jnp.float32) / PIX - 1.0
    smooth = levels[:, 0, None, None] + levels[:, 1, None, None] * coord_y[None, :, None]
    smooth = smooth + levels[:, 2, None, None] * coord_x[None, None, :]
    smooth = smooth + levels[:, 3, None, None] * coord_y[None, :, None] * coord_x[None, None, :]
    noise = 0.3 * jax.random.normal(noise_key, (VISITS, ROWS_VIS, PIX), jnp.float32)
    return (smooth + noise).astype(jnp.bfloat16)


def draw_resample(key, part):
    pixels = jnp.arange(PIX)
    identity = (pixels[:, None] == pixels[None, :]).astype(jnp.float32)
    noise = jax.random.normal(key, (VISITS, PIX, PIX), jnp.float32)
    return (identity[None] + 0.35 * noise / PIX ** 0.5).astype(jnp.bfloat16)


def draw_slot_row(key, part):
    visit_key, base_key = jax.random.split(jax.random.fold_in(key, 7))
    shape = (N_VISIT, N_CCD, N_VISIT, SLOT)
    local_visit = jax.random.randint(visit_key, shape, 0, VIS_DEV)
    base_row = jax.random.randint(base_key, shape, 0, R_DEV - TAPS + 1)
    values = (local_visit * R_DEV + base_row).astype(jnp.int32).reshape(-1)
    values = values.at[0].set(VIS_DEV * R_DEV - TAPS)
    values = values.at[values.shape[0] - 1].set(0)
    return values.reshape(shape).astype(jnp.int32)


def set_ends(entries, stream_key, low, high):
    extent = entries.shape
    index_at = [jax.random.randint(jax.random.fold_in(stream_key, axis), (), 0, extent[axis]) for axis in range(len(extent))]
    entries = entries.at[tuple(index_at)].set(low)
    longest = extent.index(max(extent))
    index_at[longest] = (index_at[longest] + 1) % extent[longest]
    return entries.at[tuple(index_at)].set(high)


def level_of(key, dims, shards, low, largest):
    gain, own = 1.0, jax.random.fold_in(key, 6)
    for axis_at, blocks in shards:
        steps = jnp.exp(jax.random.uniform(jax.random.fold_in(own, axis_at), (blocks,), jnp.float32, low / len(shards), largest / len(shards)))
        gain = gain * jnp.repeat(steps, dims[axis_at] // blocks).reshape([-1 if axis == axis_at else 1 for axis in range(len(dims))])
    return gain


def cumulative_ranks(count, slope):
    portions = [(1 << 20) // math.isqrt(grade ** slope) + 1 for grade in range(1, count + 1)]
    deviation = 1 + sum(portions) // (1 << 30)
    return np.cumsum(np.array([max(1, weight // deviation) for weight in portions]))


def ranked(rng, extent, count, skew):
    grid = cumulative_ranks(count, skew)
    ticket = jax.random.randint(jax.random.fold_in(rng, 1), extent, 0, int(grid[count - 1]))
    grade = jnp.searchsorted(jnp.asarray(grid, jnp.int32), ticket, side="right")
    return jax.random.permutation(jax.random.fold_in(rng, 2), count)[grade].astype(jnp.int32)


def setup_inputs(seed: int = 0) -> dict:
    arg_keys = jax.random.split(jax.random.key(seed), 7)
    raw_rows = draw_raw_rows(jax.random.fold_in(arg_keys[6], 71), 0)
    resample = draw_resample(jax.random.fold_in(arg_keys[6], 71), 0)
    slot_row = draw_slot_row(jax.random.fold_in(arg_keys[6], 71), 0)
    tap_weight = jnp.clip(1.0 * jax.random.uniform(arg_keys[3], (TAPS, N_VISIT, N_CCD, N_VISIT, SLOT), jnp.float32) ** level_of(arg_keys[3], (TAPS, N_VISIT, N_CCD, N_VISIT, SLOT), ((1, 8), (2, 4)), -0.2, 0.2), 0.0, 1.0)
    patch_id = set_ends(ranked(arg_keys[4], (N_VISIT, N_CCD, N_VISIT, SLOT), P_DEV, 2), jax.random.fold_in(arg_keys[4], 3), 0, P_DEV - 1).astype(jnp.int32)
    live_mask = set_ends((jax.random.randint(arg_keys[5], (N_VISIT, N_CCD, N_VISIT, SLOT), 0, 5) < 3).astype(jnp.int32), jax.random.fold_in(arg_keys[5], 1), 0, 1)
    return dict(raw_rows=raw_rows, resample=resample, slot_row=slot_row, tap_weight=tap_weight, patch_id=patch_id, live_mask=live_mask)


ridge_weight = 1.0

def chebyshev(coords):
    series = [jnp.ones_like(coords), coords]
    for degree in range(2, ORDER):
        series.append(2.0 * coords * series[-1] - series[-2])
    return jnp.stack(series[:ORDER])

def model_of(coef_rows, cheb_rows, cheb_x):
    shaped = coef_rows.reshape(coef_rows.shape[:-1] + (ORDER, ORDER))
    reduced = jnp.sum(shaped * cheb_rows[..., None, :], axis=-1)
    return jnp.einsum('...i,ip->...p', reduced, cheb_x, precision=lax.Precision.HIGHEST)

def reference(raw_rows, resample, slot_row, tap_weight, patch_id, live_mask):
    f32 = jnp.float32
    visit_devs = N_VISIT
    ccd_devs = N_CCD
    raw_split = raw_rows.reshape(visit_devs, VIS_DEV, ccd_devs, R_DEV, PIX).transpose(0, 2, 1, 3, 4)
    res_split = resample.reshape(visit_devs, VIS_DEV, PIX, PIX)
    weight_split = tap_weight.transpose(1, 2, 0, 3, 4)

    def warp_block(inputs):
        raw_part, res_part, start_part, weight_part = inputs

        def per_ccd(raw_ccd, start_ccd, weight_ccd):
            resampled = jnp.einsum('vrp,vpq->vrq', raw_ccd.astype(f32), res_part.astype(f32)).reshape(-1, PIX)
            blended = jnp.zeros(start_ccd.shape + (PIX,), f32)
            for tap_index in range(TAPS):
                blended = blended + weight_ccd[tap_index][..., None] * resampled[start_ccd + tap_index]
            return blended.astype(jnp.bfloat16)
        return jax.vmap(per_ccd)(raw_part, start_part, weight_part)
    warped = lax.map(warp_block, (raw_split, res_split, slot_row, weight_split))
    local_visit = slot_row // R_DEV
    ccd_pos = jnp.arange(ccd_devs, dtype=jnp.int32)[None, :, None, None]
    src_pos = jnp.arange(visit_devs, dtype=jnp.int32)[:, None, None, None]
    row_pos = ccd_pos * R_DEV + slot_row % R_DEV
    global_visit = src_pos * VIS_DEV + local_visit
    coord_y = (2 * row_pos + TAPS).astype(f32) / (R_DEV * ccd_devs) - 1.0
    cheb_y = jnp.moveaxis(chebyshev(coord_y), 0, -1)
    cheb_x = chebyshev((2 * jnp.arange(PIX) + 1).astype(f32) / PIX - 1.0)
    gram_x = jnp.dot(cheb_x, cheb_x.T, precision=lax.Precision.HIGHEST)
    live_float = live_mask.astype(f32)
    codes = patch_id + P_DEV * (1 - live_mask)
    visit_hot = (local_visit[..., None] == jnp.arange(VIS_DEV, dtype=jnp.int32)).astype(f32)

    def design_block(inputs):
        hot_part, cheb_part, live_part = inputs
        outer = cheb_part[..., :, None] * cheb_part[..., None, :] * live_part[..., None, None]
        outer = outer.reshape(outer.shape[:-2] + (ORDER * ORDER,))
        return jnp.einsum('cnsv,cnsm->vm', hot_part, outer, precision=lax.Precision.HIGHEST)
    design = lax.map(design_block, (visit_hot, cheb_y, live_float)).reshape(VISITS, ORDER, ORDER)
    gram = jnp.einsum('ac,vbd->vabcd', gram_x, design).reshape(VISITS, NTERM, NTERM)
    gram = gram + ridge_weight * jnp.eye(NTERM, dtype=f32)
    factor = jnp.linalg.cholesky(gram)
    offsets = jnp.zeros((VISITS, NTERM), f32)
    codes_owner = codes.transpose(2, 1, 0, 3)
    background = None
    for sweep in range(ITERS):

        def correct_block(inputs):
            warped_part, visit_part, cheb_part = inputs
            model = model_of(offsets[visit_part], cheb_part, cheb_x)
            return (warped_part.astype(f32) - model).astype(jnp.bfloat16)
        corrected = lax.map(correct_block, (warped, global_visit, cheb_y))
        corrected_owner = corrected.transpose(2, 1, 0, 3, 4)

        def consensus_block(inputs):
            rows_part, code_part = inputs

            def per_ccd(rows_ccd, code_ccd):
                patch_hot = (code_ccd[..., None] == jnp.arange(P_DEV, dtype=jnp.int32)).astype(f32)
                sums = jnp.einsum('nsk,nsq->kq', patch_hot, rows_ccd.astype(f32))
                counts = jnp.sum(patch_hot, axis=(0, 1))
                patch_bg = sums / (counts + 1.0)[:, None]
                shared = patch_bg.astype(jnp.bfloat16).astype(f32)
                returned = jnp.einsum('nsk,kq->nsq', patch_hot, shared).astype(jnp.bfloat16)
                return (patch_bg, returned)
            return jax.vmap(per_ccd)(rows_part, code_part)
        patch_bgs, returned = lax.map(consensus_block, (corrected_owner, codes_owner))
        background = patch_bgs.reshape(PATCHES, PIX)
        matched = returned.transpose(2, 1, 0, 3, 4)

        def moment_block(inputs):
            warped_part, matched_part, live_part, cheb_part, hot_part = inputs
            resid = (warped_part.astype(f32) - matched_part.astype(f32)) * live_part[..., None]
            projected = jnp.einsum('...p,ip->...i', resid, cheb_x, precision=lax.Precision.HIGHEST)
            outer = projected[..., :, None] * cheb_part[..., None, :]
            outer = outer.reshape(outer.shape[:-2] + (ORDER * ORDER,))
            return jnp.einsum('cnsv,cnsm->vm', hot_part, outer, precision=lax.Precision.HIGHEST)
        moments = lax.map(moment_block, (warped, matched, live_float, cheb_y, visit_hot)).reshape(VISITS, NTERM)
        offsets = jax.scipy.linalg.cho_solve((factor, True), moments[..., None])[..., 0]
    return (offsets, background)
```

```python
import functools
import jax
import jax.numpy as jnp
import numpy as np
from jax import lax
from jax.experimental import pallas as pl
from jax.experimental.pallas import tpu as pltpu
from jax.sharding import PartitionSpec as P

ORDER = 8
TAPS = 4
P_DEV = 16
LANES = 128
ROW_BLOCK = 256

ridge_weight = 1.0

MESH = pl.DeviceIdType.MESH
HIGH = lax.Precision.HIGHEST
F32 = jnp.float32
BF16 = jnp.bfloat16
NT = (((1,), (1,)), ((), ()))
NN = (((1,), (0,)), ((), ()))


def basis_constants(pixels, vis_local):
    coord = (2 * np.arange(pixels) + 1) / pixels - 1.0
    rows = [np.ones_like(coord), coord]
    for _ in range(2, ORDER):
        rows.append(2.0 * coord * rows[-1] - rows[-2])
    cheb = np.stack(rows)
    lam, vec = np.linalg.eigh(cheb @ cheb.T)
    used = np.arange(LANES) < vis_local * ORDER
    term = np.arange(LANES) % ORDER
    fold = (term[None] == np.arange(ORDER)[:, None]) * used
    unrot = vec[:, term] * used
    lam_lane = np.broadcast_to(lam[term] * used, (ORDER, LANES))
    wide = np.zeros((4 * ORDER, pixels))
    wide[:ORDER] = vec.T @ cheb
    wide[ORDER : 2 * ORDER, :LANES] = fold
    wide[2 * ORDER : 3 * ORDER, :LANES] = unrot
    wide[3 * ORDER :, :LANES] = lam_lane
    return wide.astype(np.float32)


def dot(a, b, dims, precision=None):
    return lax.dot_general(a, b, dims, precision=precision, preferred_element_type=F32)


def split(x, parts):
    out = []
    for _ in range(parts):
        head = x.astype(BF16)
        out.append(head)
        x = x - head.astype(F32)
    return out


def iota(shape, dim):
    return lax.broadcasted_iota(jnp.int32, shape, dim)


def kernel(
    n_v, n_c, vis_local,
    slot_ref, tap_ref, patch_ref, live_ref, const_ref, raw_hbm, res_hbm,
    off_ref, bg_ref,
    raw_ref, res_ref, iscr, tscr, wscr, tw_ref, d_ref, s_ref, sext_ref, s1_ref,
    pa_ref, q_ref, s_recv, m_recv, m2_recv, pa_recv, q_recv, s1_recv,
    load_sem, ssend, srecv, asend, arecv, bsend, brecv, csend, crecv, dsend, drecv, gsend, grecv,
):
    vi, ci = lax.axis_index("visit"), lax.axis_index("ccd")
    rows = raw_ref.shape[1]
    slots = slot_ref.shape[1]
    npk = n_v * P_DEV
    nvb = vis_local * ORDER
    v_peer = lambda step: (lax.rem(vi + step, n_v), ci)
    c_peer = lambda step: (vi, lax.rem(ci + step, n_c))

    barrier = pltpu.get_barrier_semaphore()
    for step in range(1, n_v):
        pl.semaphore_signal(barrier, inc=1, device_id=v_peer(step), device_id_type=MESH)
    for step in range(1, n_c):
        pl.semaphore_signal(barrier, inc=1, device_id=c_peer(step), device_id_type=MESH)
    raw_load = pltpu.make_async_copy(raw_hbm, raw_ref, load_sem.at[0])
    raw_load.start()
    res_load = pltpu.make_async_copy(res_hbm, res_ref, load_sem.at[1])
    res_load.start()

    def over_visits(src_of, dst, send, recv):
        copies = []
        for step in range(1, n_v):
            copy = pltpu.make_async_remote_copy(
                src_ref=src_of(step), dst_ref=dst.at[step],
                send_sem=send.at[step], recv_sem=recv.at[step],
                device_id=v_peer(step), device_id_type=MESH,
            )
            copy.start()
            copies.append(copy)
        return copies

    def over_ccd(buf, send, recv):
        copies = []
        for step in range(1, n_c):
            copy = pltpu.make_async_remote_copy(
                src_ref=buf.at[ci], dst_ref=buf.at[ci],
                send_sem=send.at[step], recv_sem=recv.at[ci],
                device_id=c_peer(step), device_id_type=MESH,
            )
            copy.start()
            copies.append(copy)
        return copies

    def total_over_ccd(buf, send, recv):
        for step in range(1, n_c):
            sender = lax.rem(ci + n_c - step, n_c)
            pltpu.make_async_remote_copy(
                src_ref=buf.at[sender], dst_ref=buf.at[sender],
                send_sem=send.at[step], recv_sem=recv.at[sender],
                device_id=c_peer(step), device_id_type=MESH,
            ).wait_recv()
        total = buf[0]
        for c in range(1, n_c):
            total = total + buf[c]
        return total

    start = slot_ref[...]
    vis = jnp.zeros_like(start)
    for v in range(1, vis_local):
        vis = vis + (start >= v * rows).astype(jnp.int32)
    base = start - vis * rows
    live = live_ref[...] > 0
    patch = patch_ref[...]
    iscr[0] = jnp.where(live, vis * P_DEV + patch, -1)
    iscr[1] = base
    iscr[2] = jnp.where(live, iota(start.shape, 0) * P_DEV + patch, -1)
    iscr[3] = jnp.where(live, vis, -1)
    coord = (2 * (ci * rows + base) + TAPS).astype(F32) / float(rows * n_c) - 1.0
    older, newer = jnp.ones_like(coord), coord
    for degree in range(2 * ORDER):
        tscr[:, degree, :] = older
        older, newer = newer, 2.0 * coord * newer - older

    tw_ref[...] = jnp.zeros_like(tw_ref)
    d_ref[...] = jnp.zeros_like(d_ref)
    s_ref[...] = jnp.zeros_like(s_ref)
    row_at = iota((ROW_BLOCK, slots), 0)

    def chunk(j, carry):
        at = pl.ds(j, 1)
        first = iscr[1, at, :]
        vis_j = iscr[3, at, :]
        weights = [tap_ref[t, at, :] for t in range(TAPS)]
        cheb = tscr[j]
        hot = jnp.where(iota((vis_local * P_DEV, slots), 0) == iscr[0, at, :], 1.0, 0.0).astype(BF16)
        cheb_v = jnp.concatenate(
            [jnp.where(vis_j == v, cheb[:ORDER], 0.0) for v in range(vis_local)], axis=0
        )
        tv = split(cheb_v, 3)
        lhs = jnp.concatenate([hot, tv[0], tv[1]], axis=0)
        hots = vis_local * P_DEV
        for block in range(0, rows, ROW_BLOCK):
            gap = row_at - (first - block)
            taps = jnp.zeros((ROW_BLOCK, slots), F32)
            for t in range(TAPS):
                taps = jnp.where(gap == t, weights[t], taps)
            prod = dot(lhs, taps.astype(BF16), NT)
            for v in range(vis_local):
                wscr[v, pl.ds(pl.multiple_of(j * P_DEV, P_DEV), P_DEV), block : block + ROW_BLOCK] = (
                    prod[v * P_DEV : (v + 1) * P_DEV].astype(BF16)
                )
            tw_ref[:, block : block + ROW_BLOCK] += prod[hots : hots + nvb] + prod[hots + nvb :]
        member = jnp.where(iota((npk, slots), 0) == iscr[2, at, :], 1.0, 0.0).astype(BF16)
        design = dot(jnp.concatenate(tv, axis=0), member, NT)
        d_ref[...] += design[:nvb] + design[nvb : 2 * nvb] + design[2 * nvb :]
        of_visit = jnp.where((iota((LANES, slots), 0) >> 3) == vis_j, 1.0, 0.0).astype(BF16)
        sums = dot(jnp.concatenate(split(cheb, 3), axis=0), of_visit, NT)
        s_ref[...] += sums[: 2 * ORDER] + sums[2 * ORDER : 4 * ORDER] + sums[4 * ORDER :]
        return carry

    lax.fori_loop(0, n_v, chunk, 0)

    pl.semaphore_wait(barrier, n_v + n_c - 2)
    s_recv[ci] = s_ref[...]
    sent_s = over_ccd(s_recv, ssend, srecv)

    raw_load.wait()
    res_load.wait()
    tw = jnp.concatenate(split(tw_ref[...], 2), axis=0)
    sums1 = jnp.zeros((npk, raw_ref.shape[2]), F32)
    row_sums = []
    for v in range(vis_local):
        by_patch = dot(wscr[v], raw_ref[v], NN)
        by_term = dot(tw, raw_ref[v], NN)
        by_term = (by_term[:nvb] + by_term[nvb:])[v * ORDER : (v + 1) * ORDER]
        mixed = jnp.concatenate([by_patch, by_term, jnp.zeros_like(by_term)], axis=0)
        high, low = split(mixed, 2)
        warped = dot(high, res_ref[v], NN) + dot(low, res_ref[v], NN)
        sums1 = sums1 + warped[:npk]
        row_sums.append(warped[npk : npk + ORDER])
    s1_ref[...] = sums1
    cx = const_ref[:ORDER]
    design = d_ref[...]
    count = jnp.zeros((1, npk), F32)
    for v in range(vis_local):
        count = count + design[v * ORDER : v * ORDER + 1]
    pa_ref[:ORDER] = dot(cx, sums1, NT, HIGH)
    pa_ref[ORDER:] = jnp.broadcast_to(count, (ORDER, npk))
    sent_a = over_visits(lambda step: pa_ref, pa_recv, asend, arecv)

    def owner_rows(step):
        owner = lax.rem(vi + step, n_v)
        return s1_ref.at[pl.ds(pl.multiple_of(owner * P_DEV, P_DEV), P_DEV)]

    sent_g = over_visits(owner_rows, s1_recv, gsend, grecv)

    lane_visit = iota((ORDER, LANES), 1) >> 3

    def own_blocks(full):
        total = jnp.zeros((ORDER, LANES), F32)
        for v in range(vis_local):
            total = total + jnp.where(lane_visit == v, full[v * ORDER : (v + 1) * ORDER], 0.0)
        return total

    def repeat(x):
        return jnp.concatenate([x] * (LANES // ORDER), axis=0)

    warped_moment = own_blocks(dot(jnp.concatenate(row_sums, axis=0), repeat(cx), NT, HIGH))

    s_total = total_over_ccd(s_recv, ssend, srecv)
    s_ref[...] = s_total
    for q in range(2 * ORDER - 1):
        degree = abs(q - (ORDER - 1))
        sext_ref[q : q + 1] = s_ref[degree : degree + 1]
    lam = const_ref[3 * ORDER :, :LANES]
    sub = iota((ORDER, LANES), 0)
    system = []
    for b in range(ORDER):
        mean = 0.5 * (s_ref[b : b + ORDER] + sext_ref[ORDER - 1 - b : 2 * ORDER - 1 - b])
        system.append(lam * mean + jnp.where(sub == b, ridge_weight, 0.0))
    inverse = list(system)
    for k in range(ORDER):
        pivot = 1.0 / inverse[k][k : k + 1]
        off = jnp.where(sub == k, 0.0, inverse[k])
        for c in range(ORDER):
            if c != k:
                row = inverse[c][k : k + 1] * pivot
                inverse[c] = jnp.where(sub == k, row, inverse[c] - off * row)
        inverse[k] = jnp.where(sub == k, pivot, -off * pivot)

    def times(columns, x):
        total = columns[0] * x[0:1]
        for b in range(1, ORDER):
            total = total + columns[b] * x[b : b + 1]
        return total

    def solve(rhs):
        guess = times(inverse, rhs)
        return guess + times(inverse, rhs - times(system, guess))

    def by_term(coefs, fold):
        spread = jnp.concatenate([jnp.where(lane_visit == v, coefs, 0.0) for v in range(vis_local)], axis=0)
        return dot(fold, spread, NT, HIGH)

    for copy in sent_a:
        copy.wait_recv()
    arrived = pa_ref[...]
    for step in range(1, n_v):
        arrived = arrived + pa_recv[step]
    per_slot = 1.0 / (arrived[ORDER : ORDER + 1] + 1.0)
    projected = arrived[:ORDER] * per_slot
    m_recv[ci] = warped_moment - own_blocks(dot(design, repeat(projected), NT, HIGH))
    sent_b = over_ccd(m_recv, bsend, brecv)
    moment = total_over_ccd(m_recv, bsend, brecv)
    coefs = solve(moment)

    q_ref[...] = dot(by_term(coefs, const_ref[ORDER : 2 * ORDER, :LANES]), design, NN, HIGH)
    sent_c = over_visits(lambda step: q_ref, q_recv, csend, crecv)
    for copy in sent_c:
        copy.wait_recv()
    model = q_ref[...]
    for step in range(1, n_v):
        model = model + q_recv[step]
    m2_recv[ci] = lam * own_blocks(dot(design, repeat(model * per_slot), NT, HIGH))
    sent_d = over_ccd(m2_recv, dsend, drecv)

    mine = iota((P_DEV, npk), 1) == iota((P_DEV, npk), 0) + vi * P_DEV
    scale = jnp.where(mine, per_slot, 0.0)
    for copy in sent_g:
        copy.wait_recv()
    own = s1_ref[pl.ds(pl.multiple_of(vi * P_DEV, P_DEV), P_DEV)]
    for step in range(1, n_v):
        own = own + s1_recv[step]
    model_own = dot(dot(scale, model, NT, HIGH), cx, NN, HIGH)
    bg_ref[...] = own * jnp.sum(scale, axis=1, keepdims=True) - model_own

    moment = moment + total_over_ccd(m2_recv, dsend, drecv)
    off_ref[...] = by_term(solve(moment), const_ref[2 * ORDER : 3 * ORDER, :LANES])
    for copy in sent_s + sent_a + sent_b + sent_c + sent_d + sent_g:
        copy.wait_send()


def per_device(raw_rows, resample, slot_row, tap_weight, patch_id, live_mask):
    n_v, n_c = lax.axis_size("visit"), lax.axis_size("ccd")
    vis_local, rows, pixels = raw_rows.shape
    slots = slot_row.shape[3]
    npk, nvb = n_v * P_DEV, vis_local * ORDER
    consts = jnp.asarray(basis_constants(pixels, vis_local))
    vmem = pl.BlockSpec(memory_space=pltpu.VMEM)
    hbm = pl.BlockSpec(memory_space=pl.ANY)
    dma = pltpu.SemaphoreType.DMA
    coefs, background = pl.pallas_call(
        functools.partial(kernel, n_v, n_c, vis_local),
        out_shape=(
            jax.ShapeDtypeStruct((ORDER, nvb), F32),
            jax.ShapeDtypeStruct((P_DEV, pixels), F32),
        ),
        in_specs=[vmem] * 5 + [hbm] * 2,
        out_specs=(vmem, vmem),
        scratch_shapes=[
            pltpu.VMEM((vis_local, rows, pixels), BF16),
            pltpu.VMEM((vis_local, pixels, pixels), BF16),
            pltpu.VMEM((4, n_v, slots), jnp.int32),
            pltpu.VMEM((n_v, 2 * ORDER, slots), F32),
            pltpu.VMEM((vis_local, npk, rows), BF16),
            pltpu.VMEM((nvb, rows), F32),
            pltpu.VMEM((nvb, npk), F32),
            pltpu.VMEM((2 * ORDER, LANES), F32),
            pltpu.VMEM((2 * ORDER, LANES), F32),
            pltpu.VMEM((npk, pixels), F32),
            pltpu.VMEM((2 * ORDER, npk), F32),
            pltpu.VMEM((ORDER, npk), F32),
            pltpu.VMEM((n_c, 2 * ORDER, LANES), F32),
            pltpu.VMEM((n_c, ORDER, LANES), F32),
            pltpu.VMEM((n_c, ORDER, LANES), F32),
            pltpu.VMEM((n_v, 2 * ORDER, npk), F32),
            pltpu.VMEM((n_v, ORDER, npk), F32),
            pltpu.VMEM((n_v, P_DEV, pixels), F32),
            dma((2,)),
            dma((n_c,)), dma((n_c,)),
            dma((n_v,)), dma((n_v,)),
            dma((n_c,)), dma((n_c,)),
            dma((n_v,)), dma((n_v,)),
            dma((n_c,)), dma((n_c,)),
            dma((n_v,)), dma((n_v,)),
        ],
        compiler_params=pltpu.CompilerParams(
            collective_id=0, has_side_effects=True, vmem_limit_bytes=48 * 1024 * 1024
        ),
    )(slot_row[0, 0], tap_weight[:, 0, 0], patch_id[0, 0], live_mask[0, 0], consts, raw_rows, resample)
    offsets = coefs.reshape(ORDER, vis_local, ORDER).transpose(1, 0, 2).reshape(vis_local, ORDER * ORDER)
    return (offsets, background)


def solution(mesh):
    in_specs = (
        P("visit", "ccd", None),
        P("visit", None, None),
        P("visit", "ccd", None, None),
        P(None, "visit", "ccd", None, None),
        P("visit", "ccd", None, None),
        P("visit", "ccd", None, None),
    )
    out_specs = (P("visit", None), P(("visit", "ccd"), None))
    return jax.shard_map(
        per_device, mesh=mesh, in_specs=in_specs, out_specs=out_specs, check_vma=False
    )
```

```python
import functools
import jax
import jax.numpy as jnp
import numpy as np
from jax import lax
from jax.experimental import pallas as pl
from jax.experimental.pallas import tpu as pltpu
from jax.sharding import PartitionSpec as P

ORDER = 8
TAPS = 4
P_DEV = 16
LANES = 128
ROW_BLOCK = 256

ridge_weight = 1.0

MESH = pl.DeviceIdType.MESH
F32 = jnp.float32
BF16 = jnp.bfloat16
NT = (((1,), (1,)), ((), ()))
NN = (((1,), (0,)), ((), ()))


def basis_constants(pixels, vis_local):
    coord = (2 * np.arange(pixels) + 1) / pixels - 1.0
    rows = [np.ones_like(coord), coord]
    for _ in range(2, ORDER):
        rows.append(2.0 * coord * rows[-1] - rows[-2])
    cheb = np.stack(rows)
    lam, vec = np.linalg.eigh(cheb @ cheb.T)
    used = np.arange(LANES) < vis_local * ORDER
    term = np.arange(LANES) % ORDER
    fold = (term[None] == np.arange(ORDER)[:, None]) * used
    unrot = vec[:, term] * used
    lam_lane = np.broadcast_to(lam[term] * used, (ORDER, LANES))
    wide = np.zeros((4 * ORDER, pixels))
    wide[:ORDER] = vec.T @ cheb
    wide[ORDER : 2 * ORDER, :LANES] = fold
    wide[2 * ORDER : 3 * ORDER, :LANES] = unrot
    wide[3 * ORDER :, :LANES] = lam_lane
    return wide.astype(np.float32)


def dot(a, b, dims, precision=None):
    return lax.dot_general(a, b, dims, precision=precision, preferred_element_type=F32)


def split(x, parts):
    out = []
    for _ in range(parts):
        head = x.astype(BF16)
        out.append(head)
        x = x - head.astype(F32)
    return out


def wide_dot(a, b, dims):
    a_head, a_tail = split(a, 2)
    b_head, b_tail = split(b, 2)
    return dot(a_head, b_head, dims) + (dot(a_head, b_tail, dims) + dot(a_tail, b_head, dims))


def iota(shape, dim):
    return lax.broadcasted_iota(jnp.int32, shape, dim)


def kernel(
    n_v, n_c, vis_local,
    slot_hbm, tap_hbm, patch_hbm, live_hbm, const_hbm, raw_hbm, res_hbm,
    off_ref, bg_ref,
    slot_ref, tap_ref, patch_ref, live_ref, const_ref, raw_ref, res_ref, iscr, tscr, wscr, tw_ref, d_ref, s_ref, sext_ref, s1_ref,
    pa_ref, q_ref, s_recv, m_recv, m2_recv, pa_recv, q_recv, s1_recv,
    load_sem, ssend, srecv, asend, arecv, bsend, brecv, csend, crecv, dsend, drecv, gsend, grecv,
):
    vi, ci = lax.axis_index("visit"), lax.axis_index("ccd")
    rows = raw_ref.shape[1]
    slots = slot_ref.shape[3]
    npk = n_v * P_DEV
    nvb = vis_local * ORDER
    v_peer = lambda step: (lax.rem(vi + step, n_v), ci)
    c_peer = lambda step: (vi, lax.rem(ci + step, n_c))

    barrier = pltpu.get_barrier_semaphore()
    for step in range(1, n_v):
        pl.semaphore_signal(barrier, inc=1, device_id=v_peer(step), device_id_type=MESH)
    for step in range(1, n_c):
        pl.semaphore_signal(barrier, inc=1, device_id=c_peer(step), device_id_type=MESH)
    loads = []
    for src, dst in (
        (slot_hbm, slot_ref), (patch_hbm, patch_ref), (live_hbm, live_ref), (tap_hbm, tap_ref),
        (raw_hbm, raw_ref), (res_hbm, res_ref), (const_hbm, const_ref),
    ):
        loads.append(pltpu.make_async_copy(src, dst, load_sem.at[len(loads)]))
        loads[-1].start()

    def over_visits(src_of, dst, send, recv):
        copies = []
        for step in range(1, n_v):
            copy = pltpu.make_async_remote_copy(
                src_ref=src_of(step), dst_ref=dst.at[step],
                send_sem=send.at[step], recv_sem=recv.at[step],
                device_id=v_peer(step), device_id_type=MESH,
            )
            copy.start()
            copies.append(copy)
        return copies

    def over_ccd(buf, send, recv):
        copies = []
        for step in range(1, n_c):
            copy = pltpu.make_async_remote_copy(
                src_ref=buf.at[ci], dst_ref=buf.at[ci],
                send_sem=send.at[step], recv_sem=recv.at[ci],
                device_id=c_peer(step), device_id_type=MESH,
            )
            copy.start()
            copies.append(copy)
        return copies

    def total_over_ccd(buf, send, recv):
        for step in range(1, n_c):
            sender = lax.rem(ci + n_c - step, n_c)
            pltpu.make_async_remote_copy(
                src_ref=buf.at[sender], dst_ref=buf.at[sender],
                send_sem=send.at[step], recv_sem=recv.at[sender],
                device_id=c_peer(step), device_id_type=MESH,
            ).wait_recv()
        total = buf[0]
        for c in range(1, n_c):
            total = total + buf[c]
        return total

    for load in loads[:4]:
        load.wait()
    start = slot_ref[0, 0]
    vis = jnp.zeros_like(start)
    for v in range(1, vis_local):
        vis = vis + (start >= v * rows).astype(jnp.int32)
    base = start - vis * rows
    live = live_ref[0, 0] > 0
    patch = patch_ref[0, 0]
    iscr[0] = jnp.where(live, vis * P_DEV + patch, -1)
    iscr[1] = base
    iscr[2] = jnp.where(live, iota(start.shape, 0) * P_DEV + patch, -1)
    iscr[3] = jnp.where(live, vis, -1)
    coord = (2 * (ci * rows + base) + TAPS).astype(F32) / float(rows * n_c) - 1.0
    older, newer = jnp.ones_like(coord), coord
    for degree in range(2 * ORDER):
        tscr[:, degree, :] = older
        older, newer = newer, 2.0 * coord * newer - older

    tw_ref[...] = jnp.zeros_like(tw_ref)
    d_ref[...] = jnp.zeros_like(d_ref)
    s_ref[...] = jnp.zeros_like(s_ref)
    row_at = iota((ROW_BLOCK, slots), 0).astype(F32).astype(BF16)
    group = 2 if n_v % 2 == 0 else 1
    hots = vis_local * P_DEV

    def chunk(step, carry):
        tops, terms, marks = [], [], []
        for part in range(group):
            j = step * group + part
            at = pl.ds(j, 1)
            vis_j = iscr[3, at, :]
            cheb = tscr[j]
            hot = jnp.where(iota((hots, slots), 0) == iscr[0, at, :], 1.0, 0.0).astype(BF16)
            cheb_v = jnp.concatenate(
                [jnp.where(vis_j == v, cheb[:ORDER], 0.0) for v in range(vis_local)], axis=0
            )
            tv = split(cheb_v, 3)
            empty = jnp.zeros_like(hot)
            tops.append(jnp.concatenate([hot if p == part else empty for p in range(group)], axis=0))
            terms.append(jnp.concatenate(tv[:2], axis=0))
            first = iscr[1, at, :]
            weights = [tap_ref[t, 0, 0, at, :].astype(BF16) for t in range(TAPS)]
            marks.append((first, [jnp.broadcast_to(w, (ROW_BLOCK, slots)) for w in weights]))
            member = jnp.where(iota((npk, slots), 0) == iscr[2, at, :], 1.0, 0.0).astype(BF16)
            design = dot(jnp.concatenate(tv, axis=0), member, NT)
            d_ref[...] += design[:nvb] + design[nvb : 2 * nvb] + design[2 * nvb :]
            of_visit = jnp.where((iota((LANES, slots), 0) >> 3) == vis_j, 1.0, 0.0).astype(BF16)
            sums = dot(jnp.concatenate(split(cheb, 3), axis=0), of_visit, NT)
            s_ref[...] += sums[: 2 * ORDER] + sums[2 * ORDER : 4 * ORDER] + sums[4 * ORDER :]
        lhs = jnp.concatenate(
            [jnp.concatenate(tops, axis=1), jnp.concatenate(terms, axis=1)], axis=0
        )
        for block in range(0, rows, ROW_BLOCK):
            wide = []
            for first, weights in marks:
                near = jnp.clip(first - block, -2 * TAPS, ROW_BLOCK + TAPS)
                taps = jnp.zeros((ROW_BLOCK, slots), BF16)
                for t in range(TAPS):
                    taps = jnp.where(row_at == (near + t).astype(F32).astype(BF16), weights[t], taps)
                wide.append(taps)
            prod = dot(lhs, jnp.concatenate(wide, axis=1), NT)
            for part in range(group):
                at = pl.ds(pl.multiple_of((step * group + part) * P_DEV, P_DEV), P_DEV)
                for v in range(vis_local):
                    low = part * hots + v * P_DEV
                    wscr[v, at, block : block + ROW_BLOCK] = prod[low : low + P_DEV].astype(BF16)
            low = group * hots
            tw_ref[:, block : block + ROW_BLOCK] += prod[low : low + nvb] + prod[low + nvb :]
        return carry

    lax.fori_loop(0, n_v // group, chunk, 0)

    pl.semaphore_wait(barrier, n_v + n_c - 2)
    s_recv[ci] = s_ref[...]
    sent_s = over_ccd(s_recv, ssend, srecv)

    for load in loads[4:]:
        load.wait()
    sums1 = jnp.zeros((npk, raw_ref.shape[2]), F32)
    row_sums = []
    for v in range(vis_local):
        tw = tw_ref[v * ORDER : (v + 1) * ORDER]
        tw_high = tw.astype(BF16).astype(F32)
        tw = jnp.concatenate([tw_high, tw - tw_high], axis=0).astype(BF16)
        by_patch = dot(jnp.concatenate([wscr[v], tw], axis=0), raw_ref[v], NN)
        by_term = by_patch[npk : npk + ORDER] + by_patch[npk + ORDER :]
        mixed = jnp.concatenate([by_patch[:npk], by_term, jnp.zeros_like(by_term)], axis=0)
        high, low = split(mixed, 2)
        warped = dot(high, res_ref[v], NN) + dot(low, res_ref[v], NN)
        sums1 = sums1 + warped[:npk]
        row_sums.append(warped[npk : npk + ORDER])
    s1_ref[...] = sums1
    cx = const_ref[:ORDER]
    design = d_ref[...]
    count = jnp.zeros((1, npk), F32)
    for v in range(vis_local):
        count = count + design[v * ORDER : v * ORDER + 1]
    pa_ref[:ORDER] = wide_dot(cx, sums1, NT)
    pa_ref[ORDER:] = jnp.broadcast_to(count, (ORDER, npk))
    sent_a = over_visits(lambda step: pa_ref, pa_recv, asend, arecv)

    def owner_rows(step):
        owner = lax.rem(vi + step, n_v)
        return s1_ref.at[pl.ds(pl.multiple_of(owner * P_DEV, P_DEV), P_DEV)]

    sent_g = over_visits(owner_rows, s1_recv, gsend, grecv)

    lane_visit = iota((ORDER, LANES), 1) >> 3

    def own_blocks(full):
        total = jnp.zeros((ORDER, LANES), F32)
        for v in range(vis_local):
            total = total + jnp.where(lane_visit == v, full[v * ORDER : (v + 1) * ORDER], 0.0)
        return total

    def repeat(x):
        return jnp.concatenate([x] * (LANES // ORDER), axis=0)

    warped_moment = own_blocks(wide_dot(jnp.concatenate(row_sums, axis=0), repeat(cx), NT))

    s_total = total_over_ccd(s_recv, ssend, srecv)
    s_ref[...] = s_total
    for q in range(2 * ORDER - 1):
        degree = abs(q - (ORDER - 1))
        sext_ref[q : q + 1] = s_ref[degree : degree + 1]
    lam = const_ref[3 * ORDER :, :LANES]
    sub = iota((ORDER, LANES), 0)
    system = []
    for b in range(ORDER):
        mean = 0.5 * (s_ref[b : b + ORDER] + sext_ref[ORDER - 1 - b : 2 * ORDER - 1 - b])
        system.append(lam * mean + jnp.where(sub == b, ridge_weight, 0.0))
    inverse = list(system)
    for k in range(ORDER):
        pivot = 1.0 / inverse[k][k : k + 1]
        off = jnp.where(sub == k, 0.0, inverse[k])
        for c in range(ORDER):
            if c != k:
                row = inverse[c][k : k + 1] * pivot
                inverse[c] = jnp.where(sub == k, row, inverse[c] - off * row)
        inverse[k] = jnp.where(sub == k, pivot, -off * pivot)

    def times(columns, x):
        total = columns[0] * x[0:1]
        for b in range(1, ORDER):
            total = total + columns[b] * x[b : b + 1]
        return total

    def solve(rhs):
        guess = times(inverse, rhs)
        return guess + times(inverse, rhs - times(system, guess))

    def by_term(coefs, fold):
        spread = jnp.concatenate([jnp.where(lane_visit == v, coefs, 0.0) for v in range(vis_local)], axis=0)
        return wide_dot(fold, spread, NT)

    for copy in sent_a:
        copy.wait_recv()
    arrived = pa_ref[...]
    for step in range(1, n_v):
        arrived = arrived + pa_recv[step]
    per_slot = 1.0 / (arrived[ORDER : ORDER + 1] + 1.0)
    projected = arrived[:ORDER] * per_slot
    m_recv[ci] = warped_moment - own_blocks(wide_dot(design, repeat(projected), NT))
    sent_b = over_ccd(m_recv, bsend, brecv)
    moment = total_over_ccd(m_recv, bsend, brecv)
    coefs = solve(moment)

    q_ref[...] = wide_dot(by_term(coefs, const_ref[ORDER : 2 * ORDER, :LANES]), design, NN)
    sent_c = over_visits(lambda step: q_ref, q_recv, csend, crecv)
    for copy in sent_c:
        copy.wait_recv()
    model = q_ref[...]
    for step in range(1, n_v):
        model = model + q_recv[step]
    m2_recv[ci] = lam * own_blocks(wide_dot(design, repeat(model * per_slot), NT))
    sent_d = over_ccd(m2_recv, dsend, drecv)

    mine = iota((P_DEV, npk), 1) == iota((P_DEV, npk), 0) + vi * P_DEV
    scale = jnp.where(mine, per_slot, 0.0)
    for copy in sent_g:
        copy.wait_recv()
    own = s1_ref[pl.ds(pl.multiple_of(vi * P_DEV, P_DEV), P_DEV)]
    for step in range(1, n_v):
        own = own + s1_recv[step]
    model_own = wide_dot(wide_dot(scale, model, NT), cx, NN)
    bg_ref[...] = own * jnp.sum(scale, axis=1, keepdims=True) - model_own

    moment = moment + total_over_ccd(m2_recv, dsend, drecv)
    off_ref[...] = by_term(solve(moment), const_ref[2 * ORDER : 3 * ORDER, :LANES])
    for copy in sent_s + sent_a + sent_b + sent_c + sent_d + sent_g:
        copy.wait_send()


def per_device(raw_rows, resample, slot_row, tap_weight, patch_id, live_mask):
    n_v, n_c = lax.axis_size("visit"), lax.axis_size("ccd")
    vis_local, rows, pixels = raw_rows.shape
    slots = slot_row.shape[3]
    npk, nvb = n_v * P_DEV, vis_local * ORDER
    consts = jnp.asarray(basis_constants(pixels, vis_local))
    vmem = pl.BlockSpec(memory_space=pltpu.VMEM)
    hbm = pl.BlockSpec(memory_space=pltpu.HBM)
    dma = pltpu.SemaphoreType.DMA
    coefs, background = pl.pallas_call(
        functools.partial(kernel, n_v, n_c, vis_local),
        out_shape=(
            jax.ShapeDtypeStruct((ORDER, nvb), F32),
            jax.ShapeDtypeStruct((P_DEV, pixels), F32),
        ),
        in_specs=[hbm] * 7,
        out_specs=(vmem, vmem),
        scratch_shapes=[
            pltpu.VMEM(slot_row.shape, jnp.int32),
            pltpu.VMEM(tap_weight.shape, F32),
            pltpu.VMEM(patch_id.shape, jnp.int32),
            pltpu.VMEM(live_mask.shape, jnp.int32),
            pltpu.VMEM(consts.shape, F32),
            pltpu.VMEM(raw_rows.shape, BF16),
            pltpu.VMEM(resample.shape, BF16),
            pltpu.VMEM((4, n_v, slots), jnp.int32),
            pltpu.VMEM((n_v, 2 * ORDER, slots), F32),
            pltpu.VMEM((vis_local, npk, rows), BF16),
            pltpu.VMEM((nvb, rows), F32),
            pltpu.VMEM((nvb, npk), F32),
            pltpu.VMEM((2 * ORDER, LANES), F32),
            pltpu.VMEM((2 * ORDER, LANES), F32),
            pltpu.VMEM((npk, pixels), F32),
            pltpu.VMEM((2 * ORDER, npk), F32),
            pltpu.VMEM((ORDER, npk), F32),
            pltpu.VMEM((n_c, 2 * ORDER, LANES), F32),
            pltpu.VMEM((n_c, ORDER, LANES), F32),
            pltpu.VMEM((n_c, ORDER, LANES), F32),
            pltpu.VMEM((n_v, 2 * ORDER, npk), F32),
            pltpu.VMEM((n_v, ORDER, npk), F32),
            pltpu.VMEM((n_v, P_DEV, pixels), F32),
            dma((7,)),
            dma((n_c,)), dma((n_c,)),
            dma((n_v,)), dma((n_v,)),
            dma((n_c,)), dma((n_c,)),
            dma((n_v,)), dma((n_v,)),
            dma((n_c,)), dma((n_c,)),
            dma((n_v,)), dma((n_v,)),
        ],
        compiler_params=pltpu.CompilerParams(
            collective_id=0, has_side_effects=True, vmem_limit_bytes=62 * 1024 * 1024
        ),
    )(slot_row, tap_weight, patch_id, live_mask, consts, raw_rows, resample)
    offsets = coefs.reshape(ORDER, vis_local, ORDER).transpose(1, 0, 2).reshape(vis_local, ORDER * ORDER)
    return (offsets, background)


def solution(mesh):
    in_specs = (
        P("visit", "ccd", None),
        P("visit", None, None),
        P("visit", "ccd", None, None),
        P(None, "visit", "ccd", None, None),
        P("visit", "ccd", None, None),
        P("visit", "ccd", None, None),
    )
    out_specs = (P("visit", None), P(("visit", "ccd"), None))
    return jax.shard_map(
        per_device, mesh=mesh, in_specs=in_specs, out_specs=out_specs, check_vma=False
    )
```

```python
import functools
import jax
import jax.numpy as jnp
import numpy as np
from jax import lax
from jax.experimental import pallas as pl
from jax.experimental.pallas import tpu as pltpu
from jax.sharding import PartitionSpec as P

ORDER = 8
TAPS = 4
P_DEV = 16
LANES = 128
ROW_BLOCK = 256

ridge_weight = 1.0

MESH = pl.DeviceIdType.MESH
F32 = jnp.float32
BF16 = jnp.bfloat16
NT = (((1,), (1,)), ((), ()))
NN = (((1,), (0,)), ((), ()))


def basis_constants(pixels, vis_local):
    coord = (2 * np.arange(pixels) + 1) / pixels - 1.0
    rows = [np.ones_like(coord), coord]
    for _ in range(2, ORDER):
        rows.append(2.0 * coord * rows[-1] - rows[-2])
    cheb = np.stack(rows)
    lam, vec = np.linalg.eigh(cheb @ cheb.T)
    used = np.arange(LANES) < vis_local * ORDER
    term = np.arange(LANES) % ORDER
    fold = (term[None] == np.arange(ORDER)[:, None]) * used
    unrot = vec[:, term] * used
    lam_lane = np.broadcast_to(lam[term] * used, (ORDER, LANES))
    wide = np.zeros((3 * ORDER + ORDER * ORDER, pixels))
    wide[:ORDER] = vec.T @ cheb
    wide[ORDER : 2 * ORDER, :LANES] = fold
    wide[2 * ORDER : 3 * ORDER, :LANES] = lam_lane
    wide[3 * ORDER :, :LANES] = np.repeat(unrot, ORDER, axis=0)
    return wide.astype(np.float32)


def dot(a, b, dims, precision=None):
    return lax.dot_general(a, b, dims, precision=precision, preferred_element_type=F32)


def split(x, parts):
    out = []
    for _ in range(parts):
        head = x.astype(BF16)
        out.append(head)
        x = x - head.astype(F32)
    return out


def wide_dot(a, b, dims):
    a_head, a_tail = split(a, 2)
    b_head, b_tail = split(b, 2)
    return dot(a_head, b_head, dims) + (dot(a_head, b_tail, dims) + dot(a_tail, b_head, dims))


def iota(shape, dim):
    return lax.broadcasted_iota(jnp.int32, shape, dim)


def kernel(
    n_v, n_c, vis_local,
    slot_hbm, tap_hbm, patch_hbm, live_hbm, const_hbm, raw_hbm, res_hbm,
    out_ref,
    slot_ref, tap_ref, patch_ref, live_ref, const_ref, raw_ref, res_ref, iscr, tscr, wscr, tw_ref, d_ref, s_ref, sext_ref, s1_ref,
    pa_ref, q_ref, s_recv, m_recv, m2_recv, pa_recv, q_recv, s1_recv,
    load_sem, ssend, srecv, asend, arecv, bsend, brecv, csend, crecv, dsend, drecv, gsend, grecv,
):
    vi, ci = lax.axis_index("visit"), lax.axis_index("ccd")
    rows = raw_ref.shape[1]
    slots = slot_ref.shape[3]
    npk = n_v * P_DEV
    nvb = vis_local * ORDER
    v_peer = lambda step: (lax.rem(vi + step, n_v), ci)
    c_peer = lambda step: (vi, lax.rem(ci + step, n_c))

    barrier = pltpu.get_barrier_semaphore()
    for step in range(1, n_v):
        pl.semaphore_signal(barrier, inc=1, device_id=v_peer(step), device_id_type=MESH)
    for step in range(1, n_c):
        pl.semaphore_signal(barrier, inc=1, device_id=c_peer(step), device_id_type=MESH)
    loads = []
    for src, dst in (
        (slot_hbm, slot_ref), (patch_hbm, patch_ref), (live_hbm, live_ref), (tap_hbm, tap_ref),
        (raw_hbm, raw_ref), (res_hbm, res_ref), (const_hbm, const_ref),
    ):
        loads.append(pltpu.make_async_copy(src, dst, load_sem.at[len(loads)]))
        loads[-1].start()

    def over_visits(src_of, dst, send, recv):
        copies = []
        for step in range(1, n_v):
            copy = pltpu.make_async_remote_copy(
                src_ref=src_of(step), dst_ref=dst.at[step],
                send_sem=send.at[step], recv_sem=recv.at[step],
                device_id=v_peer(step), device_id_type=MESH,
            )
            copy.start()
            copies.append(copy)
        return copies

    def over_ccd(buf, send, recv):
        copies = []
        for step in range(1, n_c):
            copy = pltpu.make_async_remote_copy(
                src_ref=buf.at[ci], dst_ref=buf.at[ci],
                send_sem=send.at[step], recv_sem=recv.at[ci],
                device_id=c_peer(step), device_id_type=MESH,
            )
            copy.start()
            copies.append(copy)
        return copies

    def total_over_ccd(buf, send, recv):
        for step in range(1, n_c):
            sender = lax.rem(ci + n_c - step, n_c)
            pltpu.make_async_remote_copy(
                src_ref=buf.at[sender], dst_ref=buf.at[sender],
                send_sem=send.at[step], recv_sem=recv.at[sender],
                device_id=c_peer(step), device_id_type=MESH,
            ).wait_recv()
        total = buf[0]
        for c in range(1, n_c):
            total = total + buf[c]
        return total

    for load in loads[:4]:
        load.wait()
    start = slot_ref[0, 0]
    vis = jnp.zeros_like(start)
    for v in range(1, vis_local):
        vis = vis + (start >= v * rows).astype(jnp.int32)
    base = start - vis * rows
    live = live_ref[0, 0] > 0
    patch = patch_ref[0, 0]
    iscr[0] = jnp.where(live, vis * P_DEV + patch, -1)
    iscr[1] = base
    iscr[2] = jnp.where(live, iota(start.shape, 0) * P_DEV + patch, -1)
    iscr[3] = jnp.where(live, vis, -1)
    coord = (2 * (ci * rows + base) + TAPS).astype(F32) / float(rows * n_c) - 1.0
    older, newer = jnp.ones_like(coord), coord
    for degree in range(2 * ORDER):
        tscr[:, degree, :] = older
        older, newer = newer, 2.0 * coord * newer - older

    out_ref[P_DEV:] = jnp.zeros_like(out_ref[P_DEV:])
    tw_ref[...] = jnp.zeros_like(tw_ref)
    d_ref[...] = jnp.zeros_like(d_ref)
    s_ref[...] = jnp.zeros_like(s_ref)
    row_at = iota((ROW_BLOCK, slots), 0).astype(F32).astype(BF16)
    group = 2 if n_v % 2 == 0 else 1
    hots = vis_local * P_DEV

    def chunk(step, carry):
        tops, terms, marks = [], [], []
        for part in range(group):
            j = step * group + part
            at = pl.ds(j, 1)
            vis_j = iscr[3, at, :]
            cheb = tscr[j]
            hot = jnp.where(iota((hots, slots), 0) == iscr[0, at, :], 1.0, 0.0).astype(BF16)
            cheb_v = jnp.concatenate(
                [jnp.where(vis_j == v, cheb[:ORDER], 0.0) for v in range(vis_local)], axis=0
            )
            tv = split(cheb_v, 3)
            empty = jnp.zeros_like(hot)
            tops.append(jnp.concatenate([hot if p == part else empty for p in range(group)], axis=0))
            terms.append(jnp.concatenate(tv[:2], axis=0))
            first = iscr[1, at, :]
            weights = [tap_ref[t, 0, 0, at, :].astype(BF16) for t in range(TAPS)]
            marks.append((first, [jnp.broadcast_to(w, (ROW_BLOCK, slots)) for w in weights]))
            member = jnp.where(iota((npk, slots), 0) == iscr[2, at, :], 1.0, 0.0).astype(BF16)
            design = dot(jnp.concatenate(tv, axis=0), member, NT)
            d_ref[...] += design[:nvb] + design[nvb : 2 * nvb] + design[2 * nvb :]
            of_visit = jnp.where((iota((LANES, slots), 0) >> 3) == vis_j, 1.0, 0.0).astype(BF16)
            sums = dot(jnp.concatenate(split(cheb, 3), axis=0), of_visit, NT)
            s_ref[...] += sums[: 2 * ORDER] + sums[2 * ORDER : 4 * ORDER] + sums[4 * ORDER :]
        lhs = jnp.concatenate(
            [jnp.concatenate(tops, axis=1), jnp.concatenate(terms, axis=1)], axis=0
        )
        for block in range(0, rows, ROW_BLOCK):
            wide = []
            for first, weights in marks:
                near = jnp.clip(first - block, -2 * TAPS, ROW_BLOCK + TAPS)
                taps = jnp.zeros((ROW_BLOCK, slots), BF16)
                for t in range(TAPS):
                    taps = jnp.where(row_at == (near + t).astype(F32).astype(BF16), weights[t], taps)
                wide.append(taps)
            prod = dot(lhs, jnp.concatenate(wide, axis=1), NT)
            for part in range(group):
                at = pl.ds(pl.multiple_of((step * group + part) * P_DEV, P_DEV), P_DEV)
                for v in range(vis_local):
                    low = part * hots + v * P_DEV
                    wscr[v, at, block : block + ROW_BLOCK] = prod[low : low + P_DEV].astype(BF16)
            low = group * hots
            tw_ref[:, block : block + ROW_BLOCK] += prod[low : low + nvb] + prod[low + nvb :]
        return carry

    lax.fori_loop(0, n_v // group, chunk, 0, unroll=2)

    pl.semaphore_wait(barrier, n_v + n_c - 2)
    s_recv[ci] = s_ref[...]
    sent_s = over_ccd(s_recv, ssend, srecv)

    for load in loads[4:]:
        load.wait()
    sums1 = jnp.zeros((npk, raw_ref.shape[2]), F32)
    row_sums = []
    for v in range(vis_local):
        tw = tw_ref[v * ORDER : (v + 1) * ORDER]
        tw_high = tw.astype(BF16).astype(F32)
        tw = jnp.concatenate([tw_high, tw - tw_high], axis=0).astype(BF16)
        by_patch = dot(jnp.concatenate([wscr[v], tw], axis=0), raw_ref[v], NN)
        by_term = by_patch[npk : npk + ORDER] + by_patch[npk + ORDER :]
        mixed = jnp.concatenate([by_patch[:npk], by_term, jnp.zeros_like(by_term)], axis=0)
        high, low = split(mixed, 2)
        warped = dot(high, res_ref[v], NN) + dot(low, res_ref[v], NN)
        sums1 = sums1 + warped[:npk]
        row_sums.append(warped[npk : npk + ORDER])
    s1_ref[...] = sums1
    cx = const_ref[:ORDER]
    design = d_ref[...]
    count = jnp.zeros((1, npk), F32)
    for v in range(vis_local):
        count = count + design[v * ORDER : v * ORDER + 1]
    pa_ref[:ORDER] = wide_dot(cx, sums1, NT)
    pa_ref[ORDER:] = jnp.broadcast_to(count, (ORDER, npk))
    sent_a = over_visits(lambda step: pa_ref, pa_recv, asend, arecv)

    def owner_rows(step):
        owner = lax.rem(vi + step, n_v)
        return s1_ref.at[pl.ds(pl.multiple_of(owner * P_DEV, P_DEV), P_DEV)]

    sent_g = over_visits(owner_rows, s1_recv, gsend, grecv)

    lane_visit = iota((ORDER, LANES), 1) >> 3

    def own_blocks(full):
        total = jnp.zeros((ORDER, LANES), F32)
        for v in range(vis_local):
            total = total + jnp.where(lane_visit == v, full[v * ORDER : (v + 1) * ORDER], 0.0)
        return total

    def repeat(x):
        return jnp.concatenate([x] * (LANES // ORDER), axis=0)

    warped_moment = own_blocks(wide_dot(jnp.concatenate(row_sums, axis=0), repeat(cx), NT))

    s_total = total_over_ccd(s_recv, ssend, srecv)
    s_ref[...] = s_total
    for q in range(2 * ORDER - 1):
        degree = abs(q - (ORDER - 1))
        sext_ref[q : q + 1] = s_ref[degree : degree + 1]
    lam = const_ref[2 * ORDER : 3 * ORDER, :LANES]
    sub = iota((ORDER, LANES), 0)
    system = []
    for b in range(ORDER):
        mean = 0.5 * (s_ref[b : b + ORDER] + sext_ref[ORDER - 1 - b : 2 * ORDER - 1 - b])
        system.append(lam * mean + jnp.where(sub == b, ridge_weight, 0.0))
    inverse = list(system)
    for k in range(ORDER):
        pivot = 1.0 / inverse[k][k : k + 1]
        off = jnp.where(sub == k, 0.0, inverse[k])
        for c in range(ORDER):
            if c != k:
                row = inverse[c][k : k + 1] * pivot
                inverse[c] = jnp.where(sub == k, row, inverse[c] - off * row)
        inverse[k] = jnp.where(sub == k, pivot, -off * pivot)

    def times(columns, x):
        total = columns[0] * x[0:1]
        for b in range(1, ORDER):
            total = total + columns[b] * x[b : b + 1]
        return total

    def solve(rhs):
        guess = times(inverse, rhs)
        return guess + times(inverse, rhs - times(system, guess))

    def by_term(coefs, fold):
        spread = jnp.concatenate([jnp.where(lane_visit == v, coefs, 0.0) for v in range(vis_local)], axis=0)
        return wide_dot(fold, spread, NT)

    for copy in sent_a:
        copy.wait_recv()
    arrived = pa_ref[...]
    for step in range(1, n_v):
        arrived = arrived + pa_recv[step]
    per_slot = 1.0 / (arrived[ORDER : ORDER + 1] + 1.0)
    projected = arrived[:ORDER] * per_slot
    m_recv[ci] = warped_moment - own_blocks(wide_dot(design, repeat(projected), NT))
    sent_b = over_ccd(m_recv, bsend, brecv)
    moment = total_over_ccd(m_recv, bsend, brecv)
    coefs = solve(moment)

    q_ref[...] = wide_dot(by_term(coefs, const_ref[ORDER : 2 * ORDER, :LANES]), design, NN)
    sent_c = over_visits(lambda step: q_ref, q_recv, csend, crecv)
    for copy in sent_c:
        copy.wait_recv()
    model = q_ref[...]
    for step in range(1, n_v):
        model = model + q_recv[step]
    m2_recv[ci] = lam * own_blocks(wide_dot(design, repeat(model * per_slot), NT))
    sent_d = over_ccd(m2_recv, dsend, drecv)

    mine = iota((P_DEV, npk), 1) == iota((P_DEV, npk), 0) + vi * P_DEV
    scale = jnp.where(mine, per_slot, 0.0)
    for copy in sent_g:
        copy.wait_recv()
    own = s1_ref[pl.ds(pl.multiple_of(vi * P_DEV, P_DEV), P_DEV)]
    for step in range(1, n_v):
        own = own + s1_recv[step]
    model_own = wide_dot(wide_dot(scale, model, NT), cx, NN)
    out_ref[:P_DEV] = own * jnp.sum(scale, axis=1, keepdims=True) - model_own

    moment = moment + total_over_ccd(m2_recv, dsend, drecv)
    coefs = solve(moment)
    spread = jnp.concatenate([jnp.where(lane_visit == v, coefs, 0.0) for v in range(vis_local)], axis=0)
    terms = wide_dot(spread, const_ref[3 * ORDER :, :LANES], NT)
    own_b = (iota(terms.shape, 1) & (ORDER - 1)) == (iota(terms.shape, 0) & (ORDER - 1))
    terms = jnp.where(own_b, terms, 0.0)
    for v in range(vis_local):
        out_ref[P_DEV + v : P_DEV + v + 1, : ORDER * ORDER] = jnp.sum(
            terms[v * ORDER : (v + 1) * ORDER], axis=0, keepdims=True
        )
    for copy in sent_s + sent_a + sent_b + sent_c + sent_d + sent_g:
        copy.wait_send()


def per_device(raw_rows, resample, slot_row, tap_weight, patch_id, live_mask):
    n_v, n_c = lax.axis_size("visit"), lax.axis_size("ccd")
    vis_local, rows, pixels = raw_rows.shape
    slots = slot_row.shape[3]
    npk, nvb = n_v * P_DEV, vis_local * ORDER
    consts = jnp.asarray(basis_constants(pixels, vis_local))
    vmem = pl.BlockSpec(memory_space=pltpu.VMEM)
    hbm = pl.BlockSpec(memory_space=pltpu.HBM)
    dma = pltpu.SemaphoreType.DMA
    packed = pl.pallas_call(
        functools.partial(kernel, n_v, n_c, vis_local),
        out_shape=jax.ShapeDtypeStruct((P_DEV + 8 * (-(-vis_local // 8)), pixels), F32),
        in_specs=[hbm] * 7,
        out_specs=vmem,
        scratch_shapes=[
            pltpu.VMEM(slot_row.shape, jnp.int32),
            pltpu.VMEM(tap_weight.shape, F32),
            pltpu.VMEM(patch_id.shape, jnp.int32),
            pltpu.VMEM(live_mask.shape, jnp.int32),
            pltpu.VMEM(consts.shape, F32),
            pltpu.VMEM(raw_rows.shape, BF16),
            pltpu.VMEM(resample.shape, BF16),
            pltpu.VMEM((4, n_v, slots), jnp.int32),
            pltpu.VMEM((n_v, 2 * ORDER, slots), F32),
            pltpu.VMEM((vis_local, npk, rows), BF16),
            pltpu.VMEM((nvb, rows), F32),
            pltpu.VMEM((nvb, npk), F32),
            pltpu.VMEM((2 * ORDER, LANES), F32),
            pltpu.VMEM((2 * ORDER, LANES), F32),
            pltpu.VMEM((npk, pixels), F32),
            pltpu.VMEM((2 * ORDER, npk), F32),
            pltpu.VMEM((ORDER, npk), F32),
            pltpu.VMEM((n_c, 2 * ORDER, LANES), F32),
            pltpu.VMEM((n_c, ORDER, LANES), F32),
            pltpu.VMEM((n_c, ORDER, LANES), F32),
            pltpu.VMEM((n_v, 2 * ORDER, npk), F32),
            pltpu.VMEM((n_v, ORDER, npk), F32),
            pltpu.VMEM((n_v, P_DEV, pixels), F32),
            dma((7,)),
            dma((n_c,)), dma((n_c,)),
            dma((n_v,)), dma((n_v,)),
            dma((n_c,)), dma((n_c,)),
            dma((n_v,)), dma((n_v,)),
            dma((n_c,)), dma((n_c,)),
            dma((n_v,)), dma((n_v,)),
        ],
        compiler_params=pltpu.CompilerParams(
            collective_id=0, has_side_effects=True, vmem_limit_bytes=62 * 1024 * 1024
        ),
    )(slot_row, tap_weight, patch_id, live_mask, consts, raw_rows, resample)
    return (packed[P_DEV : P_DEV + vis_local, : ORDER * ORDER], packed[:P_DEV])


def solution(mesh):
    in_specs = (
        P("visit", "ccd", None),
        P("visit", None, None),
        P("visit", "ccd", None, None),
        P(None, "visit", "ccd", None, None),
        P("visit", "ccd", None, None),
        P("visit", "ccd", None, None),
    )
    out_specs = (P("visit", None), P(("visit", "ccd"), None))
    return jax.shard_map(
        per_device, mesh=mesh, in_specs=in_specs, out_specs=out_specs, check_vma=False
    )
```

```python
import functools
import jax
import jax.numpy as jnp
import numpy as np
from jax import lax
from jax.experimental import pallas as pl
from jax.experimental.pallas import tpu as pltpu
from jax.sharding import PartitionSpec as P

ORDER = 8
TAPS = 4
P_DEV = 16
LANES = 128
ROW_BLOCK = 256

ridge_weight = 1.0

MESH = pl.DeviceIdType.MESH
F32 = jnp.float32
BF16 = jnp.bfloat16
NT = (((1,), (1,)), ((), ()))
NN = (((1,), (0,)), ((), ()))


def basis_constants(pixels, vis_local):
    coord = (2 * np.arange(pixels) + 1) / pixels - 1.0
    rows = [np.ones_like(coord), coord]
    for _ in range(2, ORDER):
        rows.append(2.0 * coord * rows[-1] - rows[-2])
    cheb = np.stack(rows)
    lam, vec = np.linalg.eigh(cheb @ cheb.T)
    used = np.arange(LANES) < vis_local * ORDER
    term = np.arange(LANES) % ORDER
    fold = (term[None] == np.arange(ORDER)[:, None]) * used
    unrot = vec[:, term] * used
    lam_lane = np.broadcast_to(lam[term] * used, (ORDER, LANES))
    wide = np.zeros((3 * ORDER + ORDER * ORDER, pixels))
    wide[:ORDER] = vec.T @ cheb
    wide[ORDER : 2 * ORDER, :LANES] = fold
    wide[2 * ORDER : 3 * ORDER, :LANES] = lam_lane
    wide[3 * ORDER :, :LANES] = np.repeat(unrot, ORDER, axis=0)
    return wide.astype(np.float32)


def dot(a, b, dims, precision=None):
    return lax.dot_general(a, b, dims, precision=precision, preferred_element_type=F32)


def split(x, parts):
    out = []
    for _ in range(parts):
        head = x.astype(BF16)
        out.append(head)
        x = x - head.astype(F32)
    return out


def wide_dot(a, b, dims):
    a_head, a_tail = split(a, 2)
    b_head, b_tail = split(b, 2)
    return dot(a_head, b_head, dims) + (dot(a_head, b_tail, dims) + dot(a_tail, b_head, dims))


def iota(shape, dim):
    return lax.broadcasted_iota(jnp.int32, shape, dim)


def kernel(
    n_v, n_c, vis_local,
    slot_hbm, tap_hbm, patch_hbm, live_hbm, const_hbm, raw_hbm, res_hbm,
    out_ref,
    slot_ref, tap_ref, patch_ref, live_ref, const_ref, raw_ref, res_ref, iscr, tscr, wscr, tw_ref, d_ref, s_ref, sext_ref, s1_ref,
    pa_ref, d_all, s_recv, m_recv, k_recv, pa_recv, o_recv, s1_recv,
    load_sem, ssend, srecv, asend, arecv, bsend, brecv, csend, crecv, ksend, krecv, gsend, grecv, dsend, drecv,
):
    vi, ci = lax.axis_index("visit"), lax.axis_index("ccd")
    rows = raw_ref.shape[1]
    slots = slot_ref.shape[3]
    npk = n_v * P_DEV
    nvb = vis_local * ORDER
    v_peer = lambda step: (lax.rem(vi + step, n_v), ci)
    c_peer = lambda step: (vi, lax.rem(ci + step, n_c))

    barrier = pltpu.get_barrier_semaphore()
    for step in range(1, n_v):
        pl.semaphore_signal(barrier, inc=1, device_id=v_peer(step), device_id_type=MESH)
    for step in range(1, n_c):
        pl.semaphore_signal(barrier, inc=1, device_id=c_peer(step), device_id_type=MESH)
    loads = []
    for src, dst in (
        (slot_hbm, slot_ref), (patch_hbm, patch_ref), (live_hbm, live_ref), (tap_hbm, tap_ref),
        (raw_hbm, raw_ref), (res_hbm, res_ref), (const_hbm, const_ref),
    ):
        loads.append(pltpu.make_async_copy(src, dst, load_sem.at[len(loads)]))
        loads[-1].start()

    def over_visits(src_of, dst, send, recv):
        copies = []
        for step in range(1, n_v):
            copy = pltpu.make_async_remote_copy(
                src_ref=src_of(step), dst_ref=dst.at[step],
                send_sem=send.at[step], recv_sem=recv.at[step],
                device_id=v_peer(step), device_id_type=MESH,
            )
            copy.start()
            copies.append(copy)
        return copies

    def over_ccd(buf, send, recv):
        copies = []
        for step in range(1, n_c):
            copy = pltpu.make_async_remote_copy(
                src_ref=buf.at[ci], dst_ref=buf.at[ci],
                send_sem=send.at[step], recv_sem=recv.at[ci],
                device_id=c_peer(step), device_id_type=MESH,
            )
            copy.start()
            copies.append(copy)
        return copies

    def total_over_ccd(buf, send, recv):
        for step in range(1, n_c):
            sender = lax.rem(ci + n_c - step, n_c)
            pltpu.make_async_remote_copy(
                src_ref=buf.at[sender], dst_ref=buf.at[sender],
                send_sem=send.at[step], recv_sem=recv.at[sender],
                device_id=c_peer(step), device_id_type=MESH,
            ).wait_recv()
        total = buf[0]
        for c in range(1, n_c):
            total = total + buf[c]
        return total

    for load in loads[:4]:
        load.wait()
    start = slot_ref[0, 0]
    vis = jnp.zeros_like(start)
    for v in range(1, vis_local):
        vis = vis + (start >= v * rows).astype(jnp.int32)
    base = start - vis * rows
    live = live_ref[0, 0] > 0
    patch = patch_ref[0, 0]
    iscr[0] = jnp.where(live, vis * P_DEV + patch, -1)
    iscr[1] = base
    iscr[2] = jnp.where(live, iota(start.shape, 0) * P_DEV + patch, -1)
    iscr[3] = jnp.where(live, vis, -1)
    coord = (2 * (ci * rows + base) + TAPS).astype(F32) / float(rows * n_c) - 1.0
    older, newer = jnp.ones_like(coord), coord
    for degree in range(2 * ORDER):
        tscr[:, degree, :] = older
        older, newer = newer, 2.0 * coord * newer - older

    out_ref[P_DEV:] = jnp.zeros_like(out_ref[P_DEV:])
    tw_ref[...] = jnp.zeros_like(tw_ref)
    d_ref[...] = jnp.zeros_like(d_ref)
    s_ref[...] = jnp.zeros_like(s_ref)
    row_at = iota((ROW_BLOCK, slots), 0).astype(F32).astype(BF16)
    group = 2 if n_v % 2 == 0 else 1
    hots = vis_local * P_DEV

    def chunk(step, carry):
        tops, terms, marks = [], [], []
        for part in range(group):
            j = step * group + part
            at = pl.ds(j, 1)
            vis_j = iscr[3, at, :]
            cheb = tscr[j]
            hot = jnp.where(iota((hots, slots), 0) == iscr[0, at, :], 1.0, 0.0).astype(BF16)
            cheb_v = jnp.concatenate(
                [jnp.where(vis_j == v, cheb[:ORDER], 0.0) for v in range(vis_local)], axis=0
            )
            tv = split(cheb_v, 3)
            empty = jnp.zeros_like(hot)
            tops.append(jnp.concatenate([hot if p == part else empty for p in range(group)], axis=0))
            terms.append(jnp.concatenate(tv[:2], axis=0))
            first = iscr[1, at, :]
            weights = [tap_ref[t, 0, 0, at, :].astype(BF16) for t in range(TAPS)]
            marks.append((first, [jnp.broadcast_to(w, (ROW_BLOCK, slots)) for w in weights]))
            member = jnp.where(iota((npk, slots), 0) == iscr[2, at, :], 1.0, 0.0).astype(BF16)
            design = dot(jnp.concatenate(tv, axis=0), member, NT)
            d_ref[...] += design[:nvb] + design[nvb : 2 * nvb] + design[2 * nvb :]
            of_visit = jnp.where((iota((LANES, slots), 0) >> 3) == vis_j, 1.0, 0.0).astype(BF16)
            sums = dot(jnp.concatenate(split(cheb, 3), axis=0), of_visit, NT)
            s_ref[...] += sums[: 2 * ORDER] + sums[2 * ORDER : 4 * ORDER] + sums[4 * ORDER :]
        lhs = jnp.concatenate(
            [jnp.concatenate(tops, axis=1), jnp.concatenate(terms, axis=1)], axis=0
        )
        for block in range(0, rows, ROW_BLOCK):
            wide = []
            for first, weights in marks:
                near = jnp.clip(first - block, -2 * TAPS, ROW_BLOCK + TAPS)
                taps = jnp.zeros((ROW_BLOCK, slots), BF16)
                for t in range(TAPS):
                    taps = jnp.where(row_at == (near + t).astype(F32).astype(BF16), weights[t], taps)
                wide.append(taps)
            prod = dot(lhs, jnp.concatenate(wide, axis=1), NT)
            for part in range(group):
                at = pl.ds(pl.multiple_of((step * group + part) * P_DEV, P_DEV), P_DEV)
                for v in range(vis_local):
                    low = part * hots + v * P_DEV
                    wscr[v, at, block : block + ROW_BLOCK] = prod[low : low + P_DEV].astype(BF16)
            low = group * hots
            tw_ref[:, block : block + ROW_BLOCK] += prod[low : low + nvb] + prod[low + nvb :]
        return carry

    lax.fori_loop(0, n_v // group, chunk, 0, unroll=2)

    pl.semaphore_wait(barrier, n_v + n_c - 2)
    s_recv[ci] = s_ref[...]
    sent_s = over_ccd(s_recv, ssend, srecv)
    d_all[0] = d_ref[...]
    sent_d = over_visits(lambda step: d_ref, d_all, dsend, drecv)

    for load in loads[4:]:
        load.wait()
    sums1 = jnp.zeros((npk, raw_ref.shape[2]), F32)
    row_sums = []
    for v in range(vis_local):
        tw = tw_ref[v * ORDER : (v + 1) * ORDER]
        tw_high = tw.astype(BF16).astype(F32)
        tw = jnp.concatenate([tw_high, tw - tw_high], axis=0).astype(BF16)
        by_patch = dot(jnp.concatenate([wscr[v], tw], axis=0), raw_ref[v], NN)
        by_term = by_patch[npk : npk + ORDER] + by_patch[npk + ORDER :]
        mixed = jnp.concatenate([by_patch[:npk], by_term, jnp.zeros_like(by_term)], axis=0)
        high, low = split(mixed, 2)
        warped = dot(high, res_ref[v], NN) + dot(low, res_ref[v], NN)
        sums1 = sums1 + warped[:npk]
        row_sums.append(warped[npk : npk + ORDER])
    s1_ref[...] = sums1
    cx = const_ref[:ORDER]
    design = d_ref[...]
    pa_ref[...] = wide_dot(cx, sums1, NT)
    sent_a = over_visits(lambda step: pa_ref, pa_recv, asend, arecv)

    def owner_rows(step):
        owner = lax.rem(vi + step, n_v)
        return s1_ref.at[pl.ds(pl.multiple_of(owner * P_DEV, P_DEV), P_DEV)]

    sent_g = over_visits(owner_rows, s1_recv, gsend, grecv)

    lane_visit = iota((ORDER, LANES), 1) >> 3

    def own_blocks(full):
        total = jnp.zeros((ORDER, LANES), F32)
        for v in range(vis_local):
            total = total + jnp.where(lane_visit == v, full[v * ORDER : (v + 1) * ORDER], 0.0)
        return total

    def repeat(x):
        return jnp.concatenate([x] * (LANES // ORDER), axis=0)

    warped_moment = own_blocks(wide_dot(jnp.concatenate(row_sums, axis=0), repeat(cx), NT))

    s_total = total_over_ccd(s_recv, ssend, srecv)
    s_ref[...] = s_total
    for q in range(2 * ORDER - 1):
        degree = abs(q - (ORDER - 1))
        sext_ref[q : q + 1] = s_ref[degree : degree + 1]
    lam = const_ref[2 * ORDER : 3 * ORDER, :LANES]
    sub = iota((ORDER, LANES), 0)
    system = []
    for b in range(ORDER):
        mean = 0.5 * (s_ref[b : b + ORDER] + sext_ref[ORDER - 1 - b : 2 * ORDER - 1 - b])
        system.append(lam * mean + jnp.where(sub == b, ridge_weight, 0.0))
    inverse = list(system)
    for k in range(ORDER):
        pivot = 1.0 / inverse[k][k : k + 1]
        off = jnp.where(sub == k, 0.0, inverse[k])
        for c in range(ORDER):
            if c != k:
                row = inverse[c][k : k + 1] * pivot
                inverse[c] = jnp.where(sub == k, row, inverse[c] - off * row)
        inverse[k] = jnp.where(sub == k, pivot, -off * pivot)

    def times(columns, x):
        total = columns[0] * x[0:1]
        for b in range(1, ORDER):
            total = total + columns[b] * x[b : b + 1]
        return total

    def solve(rhs):
        guess = times(inverse, rhs)
        return guess + times(inverse, rhs - times(system, guess))

    def spread(coefs):
        return [jnp.where(lane_visit == v, coefs, 0.0) for v in range(vis_local)]

    for copy in sent_d:
        copy.wait_recv()
    count = jnp.zeros((1, npk), F32)
    for step in range(n_v):
        for v in range(vis_local):
            count = count + d_all[step, v * ORDER : v * ORDER + 1]
    per_slot = 1.0 / (count + 1.0)
    design_all = d_all[...].reshape(n_v * nvb, npk)
    k_recv[ci] = wide_dot(design * per_slot, design_all, NT)

    for copy in sent_a:
        copy.wait_recv()
    projected = pa_ref[...]
    for step in range(1, n_v):
        projected = projected + pa_recv[step]
    m_recv[ci] = warped_moment - own_blocks(wide_dot(design, repeat(projected * per_slot), NT))
    sent_b = over_ccd(m_recv, bsend, brecv)
    sent_k = over_ccd(k_recv, ksend, krecv)
    moment = total_over_ccd(m_recv, bsend, brecv)
    o_recv[0] = solve(moment)

    sent_c = over_visits(lambda step: o_recv.at[0], o_recv, csend, crecv)
    k_total = total_over_ccd(k_recv, ksend, krecv)
    for copy in sent_c:
        copy.wait_recv()
    coefs = []
    for step in range(n_v):
        coefs += spread(o_recv[step])
    fold = const_ref[ORDER : 2 * ORDER, :LANES]
    coefs = wide_dot(fold, jnp.concatenate(coefs, axis=0), NT)
    moment = moment + lam * own_blocks(wide_dot(k_total, repeat(coefs), NT))
    terms = wide_dot(jnp.concatenate(spread(solve(moment)), axis=0), const_ref[3 * ORDER :, :LANES], NT)
    own_b = (iota(terms.shape, 1) & (ORDER - 1)) == (iota(terms.shape, 0) & (ORDER - 1))
    terms = jnp.where(own_b, terms, 0.0)
    for v in range(vis_local):
        out_ref[P_DEV + v : P_DEV + v + 1, : ORDER * ORDER] = jnp.sum(
            terms[v * ORDER : (v + 1) * ORDER], axis=0, keepdims=True
        )
    model = wide_dot(coefs, design_all, NN)

    mine = iota((P_DEV, npk), 1) == iota((P_DEV, npk), 0) + vi * P_DEV
    scale = jnp.where(mine, per_slot, 0.0)
    for copy in sent_g:
        copy.wait_recv()
    own = s1_ref[pl.ds(pl.multiple_of(vi * P_DEV, P_DEV), P_DEV)]
    for step in range(1, n_v):
        own = own + s1_recv[step]
    model_own = wide_dot(wide_dot(scale, model, NT), cx, NN)
    out_ref[:P_DEV] = own * jnp.sum(scale, axis=1, keepdims=True) - model_own

    for copy in sent_s + sent_d + sent_a + sent_g + sent_b + sent_k + sent_c:
        copy.wait_send()


def per_device(raw_rows, resample, slot_row, tap_weight, patch_id, live_mask):
    n_v, n_c = lax.axis_size("visit"), lax.axis_size("ccd")
    vis_local, rows, pixels = raw_rows.shape
    slots = slot_row.shape[3]
    npk, nvb = n_v * P_DEV, vis_local * ORDER
    consts = jnp.asarray(basis_constants(pixels, vis_local))
    vmem = pl.BlockSpec(memory_space=pltpu.VMEM)
    hbm = pl.BlockSpec(memory_space=pltpu.HBM)
    dma = pltpu.SemaphoreType.DMA
    packed = pl.pallas_call(
        functools.partial(kernel, n_v, n_c, vis_local),
        out_shape=pltpu.VMEM((P_DEV + 8 * (-(-vis_local // 8)), pixels), F32),
        in_specs=[hbm] * 7,
        out_specs=vmem,
        scratch_shapes=[
            pltpu.VMEM(slot_row.shape, jnp.int32),
            pltpu.VMEM(tap_weight.shape, F32),
            pltpu.VMEM(patch_id.shape, jnp.int32),
            pltpu.VMEM(live_mask.shape, jnp.int32),
            pltpu.VMEM(consts.shape, F32),
            pltpu.VMEM(raw_rows.shape, BF16),
            pltpu.VMEM(resample.shape, BF16),
            pltpu.VMEM((4, n_v, slots), jnp.int32),
            pltpu.VMEM((n_v, 2 * ORDER, slots), F32),
            pltpu.VMEM((vis_local, npk, rows), BF16),
            pltpu.VMEM((nvb, rows), F32),
            pltpu.VMEM((nvb, npk), F32),
            pltpu.VMEM((2 * ORDER, LANES), F32),
            pltpu.VMEM((2 * ORDER, LANES), F32),
            pltpu.VMEM((npk, pixels), F32),
            pltpu.VMEM((ORDER, npk), F32),
            pltpu.VMEM((n_v, nvb, npk), F32),
            pltpu.VMEM((n_c, 2 * ORDER, LANES), F32),
            pltpu.VMEM((n_c, ORDER, LANES), F32),
            pltpu.VMEM((n_c, nvb, n_v * nvb), F32),
            pltpu.VMEM((n_v, ORDER, npk), F32),
            pltpu.VMEM((n_v, ORDER, LANES), F32),
            pltpu.VMEM((n_v, P_DEV, pixels), F32),
            dma((7,)),
            dma((n_c,)), dma((n_c,)),
            dma((n_v,)), dma((n_v,)),
            dma((n_c,)), dma((n_c,)),
            dma((n_v,)), dma((n_v,)),
            dma((n_c,)), dma((n_c,)),
            dma((n_v,)), dma((n_v,)),
            dma((n_v,)), dma((n_v,)),
        ],
        compiler_params=pltpu.CompilerParams(
            collective_id=0, has_side_effects=True, vmem_limit_bytes=62 * 1024 * 1024
        ),
    )(slot_row, tap_weight, patch_id, live_mask, consts, raw_rows, resample)
    return (packed[P_DEV : P_DEV + vis_local, : ORDER * ORDER], packed[:P_DEV])


def solution(mesh):
    in_specs = (
        P("visit", "ccd", None),
        P("visit", None, None),
        P("visit", "ccd", None, None),
        P(None, "visit", "ccd", None, None),
        P("visit", "ccd", None, None),
        P("visit", "ccd", None, None),
    )
    out_specs = (P("visit", None), P(("visit", "ccd"), None))
    return jax.shard_map(
        per_device, mesh=mesh, in_specs=in_specs, out_specs=out_specs, check_vma=False
    )
```

```python
import functools
import jax
import jax.numpy as jnp
import numpy as np
from jax import lax
from jax.experimental import pallas as pl
from jax.experimental.pallas import tpu as pltpu
from jax.sharding import PartitionSpec as P

ORDER = 8
TAPS = 4
P_DEV = 16
LANES = 128
ROW_BLOCK = 256

ridge_weight = 1.0

MESH = pl.DeviceIdType.MESH
F32 = jnp.float32
BF16 = jnp.bfloat16
NT = (((1,), (1,)), ((), ()))
NN = (((1,), (0,)), ((), ()))


def basis_constants(pixels, vis_local):
    coord = (2 * np.arange(pixels) + 1) / pixels - 1.0
    rows = [np.ones_like(coord), coord]
    for _ in range(2, ORDER):
        rows.append(2.0 * coord * rows[-1] - rows[-2])
    cheb = np.stack(rows)
    lam, vec = np.linalg.eigh(cheb @ cheb.T)
    used = np.arange(LANES) < vis_local * ORDER
    term = np.arange(LANES) % ORDER
    fold = (term[None] == np.arange(ORDER)[:, None]) * used
    unrot = vec[:, term] * used
    lam_lane = np.broadcast_to(lam[term] * used, (ORDER, LANES))
    wide = np.zeros((3 * ORDER + ORDER * ORDER, pixels))
    wide[:ORDER] = vec.T @ cheb
    wide[ORDER : 2 * ORDER, :LANES] = fold
    wide[2 * ORDER : 3 * ORDER, :LANES] = lam_lane
    wide[3 * ORDER :, :LANES] = np.repeat(unrot, ORDER, axis=0)
    return wide.astype(np.float32)


def dot(a, b, dims, precision=None):
    return lax.dot_general(a, b, dims, precision=precision, preferred_element_type=F32)


def split(x, parts):
    out = []
    for _ in range(parts):
        head = x.astype(BF16)
        out.append(head)
        x = x - head.astype(F32)
    return out


def wide_dot(a, b, dims):
    a_head, a_tail = split(a, 2)
    b_head, b_tail = split(b, 2)
    return dot(a_head, b_head, dims) + (dot(a_head, b_tail, dims) + dot(a_tail, b_head, dims))


def iota(shape, dim):
    return lax.broadcasted_iota(jnp.int32, shape, dim)


def kernel(
    n_v, n_c, vis_local,
    slot_hbm, tap_hbm, patch_hbm, live_hbm, const_hbm, raw_hbm, res_hbm,
    out_ref,
    slot_ref, tap_ref, patch_ref, live_ref, const_ref, raw_ref, res_ref, iscr, tscr, wscr, tw_ref, d_ref, s_ref, sext_ref, s1_ref,
    pa_ref, d_all, s_recv, m_recv, k_recv, pa_recv, o_recv, s1_recv,
    load_sem, ssend, srecv, asend, arecv, bsend, brecv, csend, crecv, ksend, krecv, gsend, grecv, dsend, drecv,
):
    vi, ci = lax.axis_index("visit"), lax.axis_index("ccd")
    rows = raw_ref.shape[1]
    slots = slot_ref.shape[3]
    npk = n_v * P_DEV
    nvb = vis_local * ORDER
    v_peer = lambda step: (lax.rem(vi + step, n_v), ci)
    c_peer = lambda step: (vi, lax.rem(ci + step, n_c))

    barrier = pltpu.get_barrier_semaphore()
    for step in range(1, n_v):
        pl.semaphore_signal(barrier, inc=1, device_id=v_peer(step), device_id_type=MESH)
    for step in range(1, n_c):
        pl.semaphore_signal(barrier, inc=1, device_id=c_peer(step), device_id_type=MESH)
    loads = []
    for src, dst in (
        (slot_hbm, slot_ref), (patch_hbm, patch_ref), (live_hbm, live_ref), (tap_hbm, tap_ref),
        (raw_hbm, raw_ref), (res_hbm, res_ref), (const_hbm, const_ref),
    ):
        loads.append(pltpu.make_async_copy(src, dst, load_sem.at[len(loads)]))
        loads[-1].start()

    def over_visits(src_of, dst, send, recv):
        copies = []
        for step in range(1, n_v):
            copy = pltpu.make_async_remote_copy(
                src_ref=src_of(step), dst_ref=dst.at[step],
                send_sem=send.at[step], recv_sem=recv.at[step],
                device_id=v_peer(step), device_id_type=MESH,
            )
            copy.start()
            copies.append(copy)
        return copies

    def over_ccd(buf, send, recv):
        copies = []
        for step in range(1, n_c):
            copy = pltpu.make_async_remote_copy(
                src_ref=buf.at[ci], dst_ref=buf.at[ci],
                send_sem=send.at[step], recv_sem=recv.at[ci],
                device_id=c_peer(step), device_id_type=MESH,
            )
            copy.start()
            copies.append(copy)
        return copies

    def total_over_ccd(buf, send, recv):
        for step in range(1, n_c):
            sender = lax.rem(ci + n_c - step, n_c)
            pltpu.make_async_remote_copy(
                src_ref=buf.at[sender], dst_ref=buf.at[sender],
                send_sem=send.at[step], recv_sem=recv.at[sender],
                device_id=c_peer(step), device_id_type=MESH,
            ).wait_recv()
        total = buf[0]
        for c in range(1, n_c):
            total = total + buf[c]
        return total

    for load in loads[:4]:
        load.wait()
    start = slot_ref[0, 0]
    vis = jnp.zeros_like(start)
    for v in range(1, vis_local):
        vis = vis + (start >= v * rows).astype(jnp.int32)
    base = start - vis * rows
    live = live_ref[0, 0] > 0
    patch = patch_ref[0, 0]
    iscr[0] = jnp.where(live, vis * P_DEV + patch, -1)
    iscr[1] = base
    iscr[2] = jnp.where(live, iota(start.shape, 0) * P_DEV + patch, -1)
    iscr[3] = jnp.where(live, vis, -1)
    coord = (2 * (ci * rows + base) + TAPS).astype(F32) / float(rows * n_c) - 1.0
    older, newer = jnp.ones_like(coord), coord
    for degree in range(2 * ORDER):
        tscr[:, degree, :] = older
        older, newer = newer, 2.0 * coord * newer - older

    out_ref[P_DEV:] = jnp.zeros_like(out_ref[P_DEV:])
    tw_ref[...] = jnp.zeros_like(tw_ref)
    d_ref[...] = jnp.zeros_like(d_ref)
    s_ref[...] = jnp.zeros_like(s_ref)
    row_at = iota((ROW_BLOCK, slots), 0).astype(F32).astype(BF16)
    group = 2 if n_v % 2 == 0 else 1
    hots = vis_local * P_DEV

    def chunk(step, carry):
        tops, terms, marks = [], [], []
        for part in range(group):
            j = step * group + part
            at = pl.ds(j, 1)
            vis_j = iscr[3, at, :]
            cheb = tscr[j]
            hot = jnp.where(iota((hots, slots), 0) == iscr[0, at, :], 1.0, 0.0).astype(BF16)
            cheb_v = jnp.concatenate(
                [jnp.where(vis_j == v, cheb[:ORDER], 0.0) for v in range(vis_local)], axis=0
            )
            tv = split(cheb_v, 3)
            empty = jnp.zeros_like(hot)
            tops.append(jnp.concatenate([hot if p == part else empty for p in range(group)], axis=0))
            terms.append(jnp.concatenate(tv[:2], axis=0))
            first = iscr[1, at, :]
            weights = [tap_ref[t, 0, 0, at, :].astype(BF16) for t in range(TAPS)]
            marks.append((first, [jnp.broadcast_to(w, (ROW_BLOCK, slots)) for w in weights]))
            member = jnp.where(iota((npk, slots), 0) == iscr[2, at, :], 1.0, 0.0).astype(BF16)
            design = dot(jnp.concatenate(tv, axis=0), member, NT)
            d_ref[...] += design[:nvb] + design[nvb : 2 * nvb] + design[2 * nvb :]
            of_visit = jnp.where((iota((LANES, slots), 0) >> 3) == vis_j, 1.0, 0.0).astype(BF16)
            sums = dot(jnp.concatenate(split(cheb, 3), axis=0), of_visit, NT)
            s_ref[...] += sums[: 2 * ORDER] + sums[2 * ORDER : 4 * ORDER] + sums[4 * ORDER :]
        lhs = jnp.concatenate(
            [jnp.concatenate(tops, axis=1), jnp.concatenate(terms, axis=1)], axis=0
        )
        for block in range(0, rows, ROW_BLOCK):
            wide = []
            for first, weights in marks:
                near = jnp.clip(first - block, -2 * TAPS, ROW_BLOCK + TAPS)
                taps = jnp.zeros((ROW_BLOCK, slots), BF16)
                for t in range(TAPS):
                    taps = jnp.where(row_at == (near + t).astype(F32).astype(BF16), weights[t], taps)
                wide.append(taps)
            prod = dot(lhs, jnp.concatenate(wide, axis=1), NT)
            for part in range(group):
                at = pl.ds(pl.multiple_of((step * group + part) * P_DEV, P_DEV), P_DEV)
                for v in range(vis_local):
                    low = part * hots + v * P_DEV
                    wscr[v, at, block : block + ROW_BLOCK] = prod[low : low + P_DEV].astype(BF16)
            low = group * hots
            tw_ref[:, block : block + ROW_BLOCK] += prod[low : low + nvb] + prod[low + nvb :]
        return carry

    lax.fori_loop(0, n_v // group, chunk, 0, unroll=2)

    pl.semaphore_wait(barrier, n_v + n_c - 2)
    s_recv[ci] = s_ref[...]
    sent_s = over_ccd(s_recv, ssend, srecv)
    d_all[0] = d_ref[...]
    sent_d = over_visits(lambda step: d_ref, d_all, dsend, drecv)

    for load in loads[4:]:
        load.wait()
    sums1 = jnp.zeros((npk, raw_ref.shape[2]), F32)
    row_sums = []
    for v in range(vis_local):
        tw = tw_ref[v * ORDER : (v + 1) * ORDER]
        tw_high = tw.astype(BF16).astype(F32)
        tw = jnp.concatenate([tw_high, tw - tw_high], axis=0).astype(BF16)
        by_patch = dot(jnp.concatenate([wscr[v], tw], axis=0), raw_ref[v], NN)
        by_term = by_patch[npk : npk + ORDER] + by_patch[npk + ORDER :]
        mixed = jnp.concatenate([by_patch[:npk], by_term, jnp.zeros_like(by_term)], axis=0)
        high, low = split(mixed, 2)
        warped = dot(high, res_ref[v], NN) + dot(low, res_ref[v], NN)
        sums1 = sums1 + warped[:npk]
        row_sums.append(warped[npk : npk + ORDER])
    s1_ref[...] = sums1
    cx = const_ref[:ORDER]
    design = d_ref[...]
    pa_ref[...] = wide_dot(cx, sums1, NT)
    sent_a = over_visits(lambda step: pa_ref, pa_recv, asend, arecv)

    def owner_rows(step):
        owner = lax.rem(vi + step, n_v)
        return s1_ref.at[pl.ds(pl.multiple_of(owner * P_DEV, P_DEV), P_DEV)]

    sent_g = over_visits(owner_rows, s1_recv, gsend, grecv)

    lane_visit = iota((ORDER, LANES), 1) >> 3

    def own_blocks(full):
        total = jnp.zeros((ORDER, LANES), F32)
        for v in range(vis_local):
            total = total + jnp.where(lane_visit == v, full[v * ORDER : (v + 1) * ORDER], 0.0)
        return total

    def repeat(x):
        return jnp.concatenate([x] * (LANES // ORDER), axis=0)

    warped_moment = own_blocks(wide_dot(jnp.concatenate(row_sums, axis=0), repeat(cx), NT))

    s_total = total_over_ccd(s_recv, ssend, srecv)
    s_ref[...] = s_total
    for q in range(2 * ORDER - 1):
        degree = abs(q - (ORDER - 1))
        sext_ref[q : q + 1] = s_ref[degree : degree + 1]
    lam = const_ref[2 * ORDER : 3 * ORDER, :LANES]
    sub = iota((ORDER, LANES), 0)
    system = []
    for b in range(ORDER):
        mean = 0.5 * (s_ref[b : b + ORDER] + sext_ref[ORDER - 1 - b : 2 * ORDER - 1 - b])
        system.append(lam * mean + jnp.where(sub == b, ridge_weight, 0.0))
    inverse = list(system)
    for k in range(ORDER):
        pivot = 1.0 / inverse[k][k : k + 1]
        off = jnp.where(sub == k, 0.0, inverse[k])
        for c in range(ORDER):
            if c != k:
                row = inverse[c][k : k + 1] * pivot
                inverse[c] = jnp.where(sub == k, row, inverse[c] - off * row)
        inverse[k] = jnp.where(sub == k, pivot, -off * pivot)

    def times(columns, x):
        total = columns[0] * x[0:1]
        for b in range(1, ORDER):
            total = total + columns[b] * x[b : b + 1]
        return total

    def solve(rhs):
        guess = times(inverse, rhs)
        return guess + times(inverse, rhs - times(system, guess))

    def spread(coefs):
        return [jnp.where(lane_visit == v, coefs, 0.0) for v in range(vis_local)]

    for copy in sent_d:
        copy.wait_recv()
    count = jnp.zeros((1, npk), F32)
    for step in range(n_v):
        for v in range(vis_local):
            count = count + d_all[step, v * ORDER : v * ORDER + 1]
    per_slot = 1.0 / (count + 1.0)
    design_all = d_all[...].reshape(n_v * nvb, npk)

    for copy in sent_a:
        copy.wait_recv()
    projected = pa_ref[...]
    for step in range(1, n_v):
        projected = projected + pa_recv[step]
    m_recv[ci] = warped_moment - own_blocks(wide_dot(design, repeat(projected * per_slot), NT))
    sent_b = over_ccd(m_recv, bsend, brecv)
    k_recv[ci] = wide_dot(design * per_slot, design_all, NT)
    sent_k = over_ccd(k_recv, ksend, krecv)
    mine = iota((P_DEV, npk), 1) == iota((P_DEV, npk), 0) + vi * P_DEV
    scale = jnp.where(mine, per_slot, 0.0)
    own_design = wide_dot(scale, design_all, NT)
    moment = total_over_ccd(m_recv, bsend, brecv)
    o_recv[0] = solve(moment)

    sent_c = over_visits(lambda step: o_recv.at[0], o_recv, csend, crecv)
    for copy in sent_g:
        copy.wait_recv()
    own = s1_ref[pl.ds(pl.multiple_of(vi * P_DEV, P_DEV), P_DEV)]
    for step in range(1, n_v):
        own = own + s1_recv[step]
    own = own * jnp.sum(scale, axis=1, keepdims=True)
    k_total = total_over_ccd(k_recv, ksend, krecv)
    for copy in sent_c:
        copy.wait_recv()
    coefs = []
    for step in range(n_v):
        coefs += spread(o_recv[step])
    fold = const_ref[ORDER : 2 * ORDER, :LANES]
    coefs = wide_dot(fold, jnp.concatenate(coefs, axis=0), NT)
    moment = moment + lam * own_blocks(wide_dot(k_total, repeat(coefs), NT))
    terms = wide_dot(jnp.concatenate(spread(solve(moment)), axis=0), const_ref[3 * ORDER :, :LANES], NT)
    own_b = (iota(terms.shape, 1) & (ORDER - 1)) == (iota(terms.shape, 0) & (ORDER - 1))
    terms = jnp.where(own_b, terms, 0.0)
    for v in range(vis_local):
        out_ref[P_DEV + v : P_DEV + v + 1, : ORDER * ORDER] = jnp.sum(
            terms[v * ORDER : (v + 1) * ORDER], axis=0, keepdims=True
        )
    out_ref[:P_DEV] = own - wide_dot(wide_dot(own_design, coefs, NT), cx, NN)

    for copy in sent_s + sent_d + sent_a + sent_g + sent_b + sent_k + sent_c:
        copy.wait_send()


def per_device(raw_rows, resample, slot_row, tap_weight, patch_id, live_mask):
    n_v, n_c = lax.axis_size("visit"), lax.axis_size("ccd")
    vis_local, rows, pixels = raw_rows.shape
    slots = slot_row.shape[3]
    npk, nvb = n_v * P_DEV, vis_local * ORDER
    consts = jnp.asarray(basis_constants(pixels, vis_local))
    vmem = pl.BlockSpec(memory_space=pltpu.VMEM)
    hbm = pl.BlockSpec(memory_space=pltpu.HBM)
    dma = pltpu.SemaphoreType.DMA
    packed = pl.pallas_call(
        functools.partial(kernel, n_v, n_c, vis_local),
        out_shape=pltpu.VMEM((P_DEV + 8 * (-(-vis_local // 8)), pixels), F32),
        in_specs=[hbm] * 7,
        out_specs=vmem,
        scratch_shapes=[
            pltpu.VMEM(slot_row.shape, jnp.int32),
            pltpu.VMEM(tap_weight.shape, F32),
            pltpu.VMEM(patch_id.shape, jnp.int32),
            pltpu.VMEM(live_mask.shape, jnp.int32),
            pltpu.VMEM(consts.shape, F32),
            pltpu.VMEM(raw_rows.shape, BF16),
            pltpu.VMEM(resample.shape, BF16),
            pltpu.VMEM((4, n_v, slots), jnp.int32),
            pltpu.VMEM((n_v, 2 * ORDER, slots), F32),
            pltpu.VMEM((vis_local, npk, rows), BF16),
            pltpu.VMEM((nvb, rows), F32),
            pltpu.VMEM((nvb, npk), F32),
            pltpu.VMEM((2 * ORDER, LANES), F32),
            pltpu.VMEM((2 * ORDER, LANES), F32),
            pltpu.VMEM((npk, pixels), F32),
            pltpu.VMEM((ORDER, npk), F32),
            pltpu.VMEM((n_v, nvb, npk), F32),
            pltpu.VMEM((n_c, 2 * ORDER, LANES), F32),
            pltpu.VMEM((n_c, ORDER, LANES), F32),
            pltpu.VMEM((n_c, nvb, n_v * nvb), F32),
            pltpu.VMEM((n_v, ORDER, npk), F32),
            pltpu.VMEM((n_v, ORDER, LANES), F32),
            pltpu.VMEM((n_v, P_DEV, pixels), F32),
            dma((7,)),
            dma((n_c,)), dma((n_c,)),
            dma((n_v,)), dma((n_v,)),
            dma((n_c,)), dma((n_c,)),
            dma((n_v,)), dma((n_v,)),
            dma((n_c,)), dma((n_c,)),
            dma((n_v,)), dma((n_v,)),
            dma((n_v,)), dma((n_v,)),
        ],
        compiler_params=pltpu.CompilerParams(
            collective_id=0, has_side_effects=True, vmem_limit_bytes=62 * 1024 * 1024
        ),
    )(slot_row, tap_weight, patch_id, live_mask, consts, raw_rows, resample)
    return (packed[P_DEV : P_DEV + vis_local, : ORDER * ORDER], packed[:P_DEV])


def solution(mesh):
    in_specs = (
        P("visit", "ccd", None),
        P("visit", None, None),
        P("visit", "ccd", None, None),
        P(None, "visit", "ccd", None, None),
        P("visit", "ccd", None, None),
        P("visit", "ccd", None, None),
    )
    out_specs = (P("visit", None), P(("visit", "ccd"), None))
    return jax.shard_map(
        per_device, mesh=mesh, in_specs=in_specs, out_specs=out_specs, check_vma=False
    )
```

```python
import functools
import jax
import jax.numpy as jnp
import numpy as np
from jax import lax
from jax.experimental import pallas as pl
from jax.experimental.pallas import tpu as pltpu
from jax.sharding import PartitionSpec as P

ORDER = 8
TAPS = 4
P_DEV = 16
LANES = 128
ROW_BLOCK = 256

ridge_weight = 1.0

MESH = pl.DeviceIdType.MESH
F32 = jnp.float32
BF16 = jnp.bfloat16
NT = (((1,), (1,)), ((), ()))
NN = (((1,), (0,)), ((), ()))


def basis_constants(pixels, vis_local):
    coord = (2 * np.arange(pixels) + 1) / pixels - 1.0
    rows = [np.ones_like(coord), coord]
    for _ in range(2, ORDER):
        rows.append(2.0 * coord * rows[-1] - rows[-2])
    cheb = np.stack(rows)
    lam, vec = np.linalg.eigh(cheb @ cheb.T)
    used = np.arange(LANES) < vis_local * ORDER
    term = np.arange(LANES) % ORDER
    fold = (term[None] == np.arange(ORDER)[:, None]) * used
    unrot = vec[:, term] * used
    lam_lane = np.broadcast_to(lam[term] * used, (ORDER, LANES))
    wide = np.zeros((3 * ORDER + ORDER * ORDER, pixels))
    wide[:ORDER] = vec.T @ cheb
    wide[ORDER : 2 * ORDER, :LANES] = fold
    wide[2 * ORDER : 3 * ORDER, :LANES] = lam_lane
    wide[3 * ORDER :, :LANES] = np.repeat(unrot, ORDER, axis=0)
    return wide.astype(np.float32)


def dot(a, b, dims, precision=None):
    return lax.dot_general(a, b, dims, precision=precision, preferred_element_type=F32)


def split(x, parts):
    out = []
    for _ in range(parts):
        head = x.astype(BF16)
        out.append(head)
        x = x - head.astype(F32)
    return out


def wide_dot(a, b, dims):
    a_head, a_tail = split(a, 2)
    b_head, b_tail = split(b, 2)
    return dot(a_head, b_head, dims) + (dot(a_head, b_tail, dims) + dot(a_tail, b_head, dims))


def iota(shape, dim):
    return lax.broadcasted_iota(jnp.int32, shape, dim)


def kernel(
    n_v, n_c, vis_local,
    slot_hbm, tap_hbm, patch_hbm, live_hbm, const_hbm, raw_hbm, res_hbm,
    out_ref,
    slot_ref, tap_ref, patch_ref, live_ref, const_ref, raw_ref, res_ref, iscr, tscr, wscr, tw_ref, d_ref, s_ref, sext_ref, s1_ref,
    pa_ref, d_all, s_recv, m_recv, k_recv, pa_recv, o_recv, s1_recv,
    load_sem, ssend, srecv, asend, arecv, bsend, brecv, csend, crecv, ksend, krecv, gsend, grecv, dsend, drecv,
):
    vi, ci = lax.axis_index("visit"), lax.axis_index("ccd")
    rows = raw_ref.shape[1]
    slots = slot_ref.shape[3]
    npk = n_v * P_DEV
    nvb = vis_local * ORDER
    v_peer = lambda step: (lax.rem(vi + step, n_v), ci)
    c_peer = lambda step: (vi, lax.rem(ci + step, n_c))

    barrier = pltpu.get_barrier_semaphore()
    for step in range(1, n_v):
        pl.semaphore_signal(barrier, inc=1, device_id=v_peer(step), device_id_type=MESH)
    for step in range(1, n_c):
        pl.semaphore_signal(barrier, inc=1, device_id=c_peer(step), device_id_type=MESH)
    loads = []
    for src, dst in (
        (slot_hbm, slot_ref), (patch_hbm, patch_ref), (live_hbm, live_ref), (tap_hbm, tap_ref),
        (raw_hbm, raw_ref), (res_hbm, res_ref), (const_hbm, const_ref),
    ):
        loads.append(pltpu.make_async_copy(src, dst, load_sem.at[len(loads)]))
        loads[-1].start()

    def over_visits(src_of, dst, send, recv):
        copies = []
        for step in range(1, n_v):
            copy = pltpu.make_async_remote_copy(
                src_ref=src_of(step), dst_ref=dst.at[step],
                send_sem=send.at[step], recv_sem=recv.at[step],
                device_id=v_peer(step), device_id_type=MESH,
            )
            copy.start()
            copies.append(copy)
        return copies

    def over_ccd(buf, send, recv):
        copies = []
        for step in range(1, n_c):
            copy = pltpu.make_async_remote_copy(
                src_ref=buf.at[ci], dst_ref=buf.at[ci],
                send_sem=send.at[step], recv_sem=recv.at[ci],
                device_id=c_peer(step), device_id_type=MESH,
            )
            copy.start()
            copies.append(copy)
        return copies

    def total_over_ccd(buf, send, recv):
        for step in range(1, n_c):
            sender = lax.rem(ci + n_c - step, n_c)
            pltpu.make_async_remote_copy(
                src_ref=buf.at[sender], dst_ref=buf.at[sender],
                send_sem=send.at[step], recv_sem=recv.at[sender],
                device_id=c_peer(step), device_id_type=MESH,
            ).wait_recv()
        total = buf[0]
        for c in range(1, n_c):
            total = total + buf[c]
        return total

    for load in loads[:4]:
        load.wait()
    start = slot_ref[0, 0]
    vis = jnp.zeros_like(start)
    for v in range(1, vis_local):
        vis = vis + (start >= v * rows).astype(jnp.int32)
    base = start - vis * rows
    live = live_ref[0, 0] > 0
    patch = patch_ref[0, 0]
    iscr[0] = jnp.where(live, vis * P_DEV + patch, -1)
    iscr[1] = base
    iscr[2] = jnp.where(live, iota(start.shape, 0) * P_DEV + patch, -1)
    iscr[3] = jnp.where(live, vis, -1)
    coord = (2 * (ci * rows + base) + TAPS).astype(F32) / float(rows * n_c) - 1.0
    older, newer = jnp.ones_like(coord), coord
    for degree in range(2 * ORDER):
        tscr[:, degree, :] = older
        older, newer = newer, 2.0 * coord * newer - older

    out_ref[P_DEV:] = jnp.zeros_like(out_ref[P_DEV:])
    tw_ref[...] = jnp.zeros_like(tw_ref)
    d_ref[...] = jnp.zeros_like(d_ref)
    s_ref[...] = jnp.zeros_like(s_ref)
    row_at = iota((ROW_BLOCK, slots), 0).astype(F32).astype(BF16)
    group = 2 if n_v % 2 == 0 else 1
    hots = vis_local * P_DEV

    def chunk(step, carry):
        tops, terms, marks = [], [], []
        for part in range(group):
            j = step * group + part
            at = pl.ds(j, 1)
            vis_j = iscr[3, at, :]
            cheb = tscr[j]
            hot = jnp.where(iota((hots, slots), 0) == iscr[0, at, :], 1.0, 0.0).astype(BF16)
            cheb_v = jnp.concatenate(
                [jnp.where(vis_j == v, cheb[:ORDER], 0.0) for v in range(vis_local)], axis=0
            )
            tv = split(cheb_v, 3)
            empty = jnp.zeros_like(hot)
            tops.append(jnp.concatenate([hot if p == part else empty for p in range(group)], axis=0))
            terms.append(jnp.concatenate(tv[:2], axis=0))
            first = iscr[1, at, :]
            weights = [tap_ref[t, 0, 0, at, :].astype(BF16) for t in range(TAPS)]
            marks.append((first, [jnp.broadcast_to(w, (ROW_BLOCK, slots)) for w in weights]))
            member = jnp.where(iota((npk, slots), 0) == iscr[2, at, :], 1.0, 0.0).astype(BF16)
            design = dot(jnp.concatenate(tv, axis=0), member, NT)
            d_ref[...] += design[:nvb] + design[nvb : 2 * nvb] + design[2 * nvb :]
            of_visit = jnp.where((iota((LANES, slots), 0) >> 3) == vis_j, 1.0, 0.0).astype(BF16)
            sums = dot(jnp.concatenate(split(cheb, 3), axis=0), of_visit, NT)
            s_ref[...] += sums[: 2 * ORDER] + sums[2 * ORDER : 4 * ORDER] + sums[4 * ORDER :]
        lhs = jnp.concatenate(
            [jnp.concatenate(tops, axis=1), jnp.concatenate(terms, axis=1)], axis=0
        )
        for block in range(0, rows, ROW_BLOCK):
            wide = []
            for first, weights in marks:
                near = jnp.clip(first - block, -2 * TAPS, ROW_BLOCK + TAPS)
                taps = jnp.zeros((ROW_BLOCK, slots), BF16)
                for t in range(TAPS):
                    taps = jnp.where(row_at == (near + t).astype(F32).astype(BF16), weights[t], taps)
                wide.append(taps)
            prod = dot(lhs, jnp.concatenate(wide, axis=1), NT)
            for part in range(group):
                at = pl.ds(pl.multiple_of((step * group + part) * P_DEV, P_DEV), P_DEV)
                for v in range(vis_local):
                    low = part * hots + v * P_DEV
                    wscr[v, at, block : block + ROW_BLOCK] = prod[low : low + P_DEV].astype(BF16)
            low = group * hots
            tw_ref[:, block : block + ROW_BLOCK] += prod[low : low + nvb] + prod[low + nvb :]
        return carry

    lax.fori_loop(0, n_v // group, chunk, 0, unroll=2)

    pl.semaphore_wait(barrier, n_v + n_c - 2)
    s_recv[ci] = s_ref[...]
    sent_s = over_ccd(s_recv, ssend, srecv)
    d_all[0] = d_ref[...]
    sent_d = over_visits(lambda step: d_ref, d_all, dsend, drecv)

    for load in loads[4:]:
        load.wait()
    cx = const_ref[:ORDER]
    cx_head, cx_tail = split(cx, 2)
    back = [dot(cx_head, res_ref[v], NT) + dot(cx_tail, res_ref[v], NT) for v in range(vis_local)]
    by_patch, by_row = [], []
    for v in range(vis_local):
        tw = tw_ref[v * ORDER : (v + 1) * ORDER]
        tw_high = tw.astype(BF16).astype(F32)
        tw = jnp.concatenate([tw_high, tw - tw_high], axis=0).astype(BF16)
        mixed = dot(jnp.concatenate([wscr[v], tw], axis=0), raw_ref[v], NN)
        by_patch.append(mixed[:npk])
        by_row.append(mixed[npk : npk + ORDER] + mixed[npk + ORDER :])
    design = d_ref[...]
    pa_ref[...] = wide_dot(jnp.concatenate(back, axis=1), jnp.concatenate(by_patch, axis=1), NT)
    sent_a = over_visits(lambda step: pa_ref, pa_recv, asend, arecv)

    lane_visit = iota((ORDER, LANES), 1) >> 3

    def own_blocks(full):
        total = jnp.zeros((ORDER, LANES), F32)
        for v in range(vis_local):
            total = total + jnp.where(lane_visit == v, full[v * ORDER : (v + 1) * ORDER], 0.0)
        return total

    def repeat(x):
        return jnp.concatenate([x] * (LANES // ORDER), axis=0)

    warped_moment = own_blocks(
        jnp.concatenate([wide_dot(by_row[v], repeat(back[v]), NT) for v in range(vis_local)], axis=0)
    )

    s_total = total_over_ccd(s_recv, ssend, srecv)
    s_ref[...] = s_total
    for q in range(2 * ORDER - 1):
        degree = abs(q - (ORDER - 1))
        sext_ref[q : q + 1] = s_ref[degree : degree + 1]
    lam = const_ref[2 * ORDER : 3 * ORDER, :LANES]
    sub = iota((ORDER, LANES), 0)
    system = []
    for b in range(ORDER):
        mean = 0.5 * (s_ref[b : b + ORDER] + sext_ref[ORDER - 1 - b : 2 * ORDER - 1 - b])
        system.append(lam * mean + jnp.where(sub == b, ridge_weight, 0.0))
    inverse = list(system)
    for k in range(ORDER):
        pivot = 1.0 / inverse[k][k : k + 1]
        off = jnp.where(sub == k, 0.0, inverse[k])
        for c in range(ORDER):
            if c != k:
                row = inverse[c][k : k + 1] * pivot
                inverse[c] = jnp.where(sub == k, row, inverse[c] - off * row)
        inverse[k] = jnp.where(sub == k, pivot, -off * pivot)

    def times(columns, x):
        total = columns[0] * x[0:1]
        for b in range(1, ORDER):
            total = total + columns[b] * x[b : b + 1]
        return total

    def solve(rhs):
        guess = times(inverse, rhs)
        return guess + times(inverse, rhs - times(system, guess))

    def spread(coefs):
        return [jnp.where(lane_visit == v, coefs, 0.0) for v in range(vis_local)]

    for copy in sent_d:
        copy.wait_recv()
    count = jnp.zeros((1, npk), F32)
    for step in range(n_v):
        for v in range(vis_local):
            count = count + d_all[step, v * ORDER : v * ORDER + 1]
    per_slot = 1.0 / (count + 1.0)
    design_all = d_all[...].reshape(n_v * nvb, npk)

    for copy in sent_a:
        copy.wait_recv()
    projected = pa_ref[...]
    for step in range(1, n_v):
        projected = projected + pa_recv[step]
    m_recv[ci] = warped_moment - own_blocks(wide_dot(design, repeat(projected * per_slot), NT))
    sent_b = over_ccd(m_recv, bsend, brecv)
    k_recv[ci] = wide_dot(design * per_slot, design_all, NT)
    sent_k = over_ccd(k_recv, ksend, krecv)
    mine = iota((P_DEV, npk), 1) == iota((P_DEV, npk), 0) + vi * P_DEV
    scale = jnp.where(mine, per_slot, 0.0)
    own_design = wide_dot(scale, design_all, NT)
    sums1 = jnp.zeros((npk, raw_ref.shape[2]), F32)
    for v in range(vis_local):
        high, low = split(by_patch[v], 2)
        sums1 = sums1 + (dot(high, res_ref[v], NN) + dot(low, res_ref[v], NN))
    s1_ref[...] = sums1

    def owner_rows(step):
        owner = lax.rem(vi + step, n_v)
        return s1_ref.at[pl.ds(pl.multiple_of(owner * P_DEV, P_DEV), P_DEV)]

    sent_g = over_visits(owner_rows, s1_recv, gsend, grecv)

    moment = total_over_ccd(m_recv, bsend, brecv)
    o_recv[0] = solve(moment)

    sent_c = over_visits(lambda step: o_recv.at[0], o_recv, csend, crecv)
    for copy in sent_g:
        copy.wait_recv()
    own = s1_ref[pl.ds(pl.multiple_of(vi * P_DEV, P_DEV), P_DEV)]
    for step in range(1, n_v):
        own = own + s1_recv[step]
    own = own * jnp.sum(scale, axis=1, keepdims=True)
    k_total = total_over_ccd(k_recv, ksend, krecv)
    for copy in sent_c:
        copy.wait_recv()
    coefs = []
    for step in range(n_v):
        coefs += spread(o_recv[step])
    fold = const_ref[ORDER : 2 * ORDER, :LANES]
    coefs = wide_dot(fold, jnp.concatenate(coefs, axis=0), NT)
    moment = moment + lam * own_blocks(wide_dot(k_total, repeat(coefs), NT))
    terms = wide_dot(jnp.concatenate(spread(solve(moment)), axis=0), const_ref[3 * ORDER :, :LANES], NT)
    own_b = (iota(terms.shape, 1) & (ORDER - 1)) == (iota(terms.shape, 0) & (ORDER - 1))
    terms = jnp.where(own_b, terms, 0.0)
    for v in range(vis_local):
        out_ref[P_DEV + v : P_DEV + v + 1, : ORDER * ORDER] = jnp.sum(
            terms[v * ORDER : (v + 1) * ORDER], axis=0, keepdims=True
        )
    out_ref[:P_DEV] = own - wide_dot(wide_dot(own_design, coefs, NT), cx, NN)

    for copy in sent_s + sent_d + sent_a + sent_g + sent_b + sent_k + sent_c:
        copy.wait_send()


def per_device(raw_rows, resample, slot_row, tap_weight, patch_id, live_mask):
    n_v, n_c = lax.axis_size("visit"), lax.axis_size("ccd")
    vis_local, rows, pixels = raw_rows.shape
    slots = slot_row.shape[3]
    npk, nvb = n_v * P_DEV, vis_local * ORDER
    consts = jnp.asarray(basis_constants(pixels, vis_local))
    vmem = pl.BlockSpec(memory_space=pltpu.VMEM)
    hbm = pl.BlockSpec(memory_space=pltpu.HBM)
    dma = pltpu.SemaphoreType.DMA
    packed = pl.pallas_call(
        functools.partial(kernel, n_v, n_c, vis_local),
        out_shape=pltpu.VMEM((P_DEV + 8 * (-(-vis_local // 8)), pixels), F32),
        in_specs=[hbm] * 7,
        out_specs=vmem,
        scratch_shapes=[
            pltpu.VMEM(slot_row.shape, jnp.int32),
            pltpu.VMEM(tap_weight.shape, F32),
            pltpu.VMEM(patch_id.shape, jnp.int32),
            pltpu.VMEM(live_mask.shape, jnp.int32),
            pltpu.VMEM(consts.shape, F32),
            pltpu.VMEM(raw_rows.shape, BF16),
            pltpu.VMEM(resample.shape, BF16),
            pltpu.VMEM((4, n_v, slots), jnp.int32),
            pltpu.VMEM((n_v, 2 * ORDER, slots), F32),
            pltpu.VMEM((vis_local, npk, rows), BF16),
            pltpu.VMEM((nvb, rows), F32),
            pltpu.VMEM((nvb, npk), F32),
            pltpu.VMEM((2 * ORDER, LANES), F32),
            pltpu.VMEM((2 * ORDER, LANES), F32),
            pltpu.VMEM((npk, pixels), F32),
            pltpu.VMEM((ORDER, npk), F32),
            pltpu.VMEM((n_v, nvb, npk), F32),
            pltpu.VMEM((n_c, 2 * ORDER, LANES), F32),
            pltpu.VMEM((n_c, ORDER, LANES), F32),
            pltpu.VMEM((n_c, nvb, n_v * nvb), F32),
            pltpu.VMEM((n_v, ORDER, npk), F32),
            pltpu.VMEM((n_v, ORDER, LANES), F32),
            pltpu.VMEM((n_v, P_DEV, pixels), F32),
            dma((7,)),
            dma((n_c,)), dma((n_c,)),
            dma((n_v,)), dma((n_v,)),
            dma((n_c,)), dma((n_c,)),
            dma((n_v,)), dma((n_v,)),
            dma((n_c,)), dma((n_c,)),
            dma((n_v,)), dma((n_v,)),
            dma((n_v,)), dma((n_v,)),
        ],
        compiler_params=pltpu.CompilerParams(
            collective_id=0, has_side_effects=True, vmem_limit_bytes=62 * 1024 * 1024
        ),
    )(slot_row, tap_weight, patch_id, live_mask, consts, raw_rows, resample)
    return (packed[P_DEV : P_DEV + vis_local, : ORDER * ORDER], packed[:P_DEV])


def solution(mesh):
    in_specs = (
        P("visit", "ccd", None),
        P("visit", None, None),
        P("visit", "ccd", None, None),
        P(None, "visit", "ccd", None, None),
        P("visit", "ccd", None, None),
        P("visit", "ccd", None, None),
    )
    out_specs = (P("visit", None), P(("visit", "ccd"), None))
    return jax.shard_map(
        per_device, mesh=mesh, in_specs=in_specs, out_specs=out_specs, check_vma=False
    )
```

```python
import functools
import jax
import jax.numpy as jnp
import numpy as np
from jax import lax
from jax.experimental import pallas as pl
from jax.experimental.pallas import tpu as pltpu
from jax.sharding import PartitionSpec as P

ORDER = 8
TAPS = 4
P_DEV = 16
LANES = 128
ROW_BLOCK = 256

ridge_weight = 1.0

MESH = pl.DeviceIdType.MESH
F32 = jnp.float32
BF16 = jnp.bfloat16
NT = (((1,), (1,)), ((), ()))
NN = (((1,), (0,)), ((), ()))


def basis_constants(pixels, vis_local):
    coord = (2 * np.arange(pixels) + 1) / pixels - 1.0
    rows = [np.ones_like(coord), coord]
    for _ in range(2, ORDER):
        rows.append(2.0 * coord * rows[-1] - rows[-2])
    cheb = np.stack(rows)
    lam, vec = np.linalg.eigh(cheb @ cheb.T)
    used = np.arange(LANES) < vis_local * ORDER
    term = np.arange(LANES) % ORDER
    fold = (term[None] == np.arange(ORDER)[:, None]) * used
    unrot = vec[:, term] * used
    lam_lane = np.broadcast_to(lam[term] * used, (ORDER, LANES))
    wide = np.zeros((3 * ORDER + ORDER * ORDER, pixels))
    wide[:ORDER] = vec.T @ cheb
    wide[ORDER : 2 * ORDER, :LANES] = fold
    wide[2 * ORDER : 3 * ORDER, :LANES] = lam_lane
    wide[3 * ORDER :, :LANES] = np.repeat(unrot, ORDER, axis=0)
    return wide.astype(np.float32)


def dot(a, b, dims, precision=None):
    return lax.dot_general(a, b, dims, precision=precision, preferred_element_type=F32)


def split(x, parts):
    out = []
    for _ in range(parts):
        head = x.astype(BF16)
        out.append(head)
        x = x - head.astype(F32)
    return out


def wide_dot(a, b, dims):
    a_head, a_tail = split(a, 2)
    b_head, b_tail = split(b, 2)
    return dot(a_head, b_head, dims) + (dot(a_head, b_tail, dims) + dot(a_tail, b_head, dims))


def iota(shape, dim):
    return lax.broadcasted_iota(jnp.int32, shape, dim)


def kernel(
    n_v, n_c, vis_local,
    slot_hbm, tap_hbm, patch_hbm, live_hbm, const_hbm, raw_hbm, res_hbm,
    out_ref,
    slot_ref, tap_ref, patch_ref, live_ref, const_ref, raw_ref, res_ref, iscr, tscr, wscr, tw_ref, d_ref, s_ref, sext_ref, s1_ref,
    pa_ref, d_all, s_recv, m_recv, k_recv, pa_recv, o_recv, s1_recv,
    load_sem, ssend, srecv, asend, arecv, bsend, brecv, csend, crecv, ksend, krecv, gsend, grecv, dsend, drecv,
):
    vi, ci = lax.axis_index("visit"), lax.axis_index("ccd")
    rows = raw_ref.shape[1]
    slots = slot_ref.shape[3]
    npk = n_v * P_DEV
    nvb = vis_local * ORDER
    v_peer = lambda step: (lax.rem(vi + step, n_v), ci)
    c_peer = lambda step: (vi, lax.rem(ci + step, n_c))

    barrier = pltpu.get_barrier_semaphore()
    for step in range(1, n_v):
        pl.semaphore_signal(barrier, inc=1, device_id=v_peer(step), device_id_type=MESH)
    for step in range(1, n_c):
        pl.semaphore_signal(barrier, inc=1, device_id=c_peer(step), device_id_type=MESH)
    loads = []
    for src, dst in (
        (slot_hbm, slot_ref), (patch_hbm, patch_ref), (live_hbm, live_ref), (tap_hbm, tap_ref),
        (raw_hbm, raw_ref), (res_hbm, res_ref), (const_hbm, const_ref),
    ):
        loads.append(pltpu.make_async_copy(src, dst, load_sem.at[len(loads)]))
        loads[-1].start()

    def over_visits(src_of, dst, send, recv):
        copies = []
        for step in range(1, n_v):
            copy = pltpu.make_async_remote_copy(
                src_ref=src_of(step), dst_ref=dst.at[step],
                send_sem=send.at[step], recv_sem=recv.at[step],
                device_id=v_peer(step), device_id_type=MESH,
            )
            copy.start()
            copies.append(copy)
        return copies

    def over_ccd(buf, send, recv):
        copies = []
        for step in range(1, n_c):
            copy = pltpu.make_async_remote_copy(
                src_ref=buf.at[ci], dst_ref=buf.at[ci],
                send_sem=send.at[step], recv_sem=recv.at[ci],
                device_id=c_peer(step), device_id_type=MESH,
            )
            copy.start()
            copies.append(copy)
        return copies

    def total_over_ccd(buf, send, recv):
        for step in range(1, n_c):
            sender = lax.rem(ci + n_c - step, n_c)
            pltpu.make_async_remote_copy(
                src_ref=buf.at[sender], dst_ref=buf.at[sender],
                send_sem=send.at[step], recv_sem=recv.at[sender],
                device_id=c_peer(step), device_id_type=MESH,
            ).wait_recv()
        total = buf[0]
        for c in range(1, n_c):
            total = total + buf[c]
        return total

    for load in loads[:4]:
        load.wait()
    start = slot_ref[0, 0]
    vis = jnp.zeros_like(start)
    for v in range(1, vis_local):
        vis = vis + (start >= v * rows).astype(jnp.int32)
    base = start - vis * rows
    live = live_ref[0, 0] > 0
    patch = patch_ref[0, 0]
    iscr[0] = jnp.where(live, vis * P_DEV + patch, -1)
    iscr[1] = base
    iscr[2] = jnp.where(live, iota(start.shape, 0) * P_DEV + patch, -1)
    iscr[3] = jnp.where(live, vis, -1)
    coord = (2 * (ci * rows + base) + TAPS).astype(F32) / float(rows * n_c) - 1.0
    older, newer = jnp.ones_like(coord), coord
    for degree in range(2 * ORDER):
        tscr[:, degree, :] = older
        older, newer = newer, 2.0 * coord * newer - older

    out_ref[P_DEV:] = jnp.zeros_like(out_ref[P_DEV:])
    tw_ref[...] = jnp.zeros_like(tw_ref)
    d_ref[...] = jnp.zeros_like(d_ref)
    s_ref[...] = jnp.zeros_like(s_ref)
    row_at = iota((ROW_BLOCK, slots), 0).astype(F32).astype(BF16)
    group = 2 if n_v % 2 == 0 else 1
    hots = vis_local * P_DEV

    def chunk(step, carry):
        tops, terms, marks = [], [], []
        for part in range(group):
            j = step * group + part
            at = pl.ds(j, 1)
            vis_j = iscr[3, at, :]
            cheb = tscr[j]
            hot = jnp.where(iota((hots, slots), 0) == iscr[0, at, :], 1.0, 0.0).astype(BF16)
            cheb_v = jnp.concatenate(
                [jnp.where(vis_j == v, cheb[:ORDER], 0.0) for v in range(vis_local)], axis=0
            )
            tv = split(cheb_v, 3)
            empty = jnp.zeros_like(hot)
            tops.append(jnp.concatenate([hot if p == part else empty for p in range(group)], axis=0))
            terms.append(jnp.concatenate(tv[:2], axis=0))
            first = iscr[1, at, :]
            weights = [tap_ref[t, 0, 0, at, :].astype(BF16) for t in range(TAPS)]
            marks.append((first, [jnp.broadcast_to(w, (ROW_BLOCK, slots)) for w in weights]))
            member = jnp.where(iota((npk, slots), 0) == iscr[2, at, :], 1.0, 0.0).astype(BF16)
            design = dot(jnp.concatenate(tv, axis=0), member, NT)
            d_ref[...] += design[:nvb] + design[nvb : 2 * nvb] + design[2 * nvb :]
            of_visit = jnp.where((iota((LANES, slots), 0) >> 3) == vis_j, 1.0, 0.0).astype(BF16)
            sums = dot(jnp.concatenate(split(cheb, 3), axis=0), of_visit, NT)
            s_ref[...] += sums[: 2 * ORDER] + sums[2 * ORDER : 4 * ORDER] + sums[4 * ORDER :]
        lhs = jnp.concatenate(
            [jnp.concatenate(tops, axis=1), jnp.concatenate(terms, axis=1)], axis=0
        )
        for block in range(0, rows, ROW_BLOCK):
            wide = []
            for first, weights in marks:
                near = jnp.clip(first - block, -2 * TAPS, ROW_BLOCK + TAPS)
                taps = jnp.zeros((ROW_BLOCK, slots), BF16)
                for t in range(TAPS):
                    taps = jnp.where(row_at == (near + t).astype(F32).astype(BF16), weights[t], taps)
                wide.append(taps)
            prod = dot(lhs, jnp.concatenate(wide, axis=1), NT)
            for part in range(group):
                at = pl.ds(pl.multiple_of((step * group + part) * P_DEV, P_DEV), P_DEV)
                for v in range(vis_local):
                    low = part * hots + v * P_DEV
                    wscr[v, at, block : block + ROW_BLOCK] = prod[low : low + P_DEV].astype(BF16)
            low = group * hots
            tw_ref[:, block : block + ROW_BLOCK] += prod[low : low + nvb] + prod[low + nvb :]
        return carry

    lax.fori_loop(0, n_v // group, chunk, 0, unroll=4)

    pl.semaphore_wait(barrier, n_v + n_c - 2)
    s_recv[ci] = s_ref[...]
    sent_s = over_ccd(s_recv, ssend, srecv)
    d_all[0] = d_ref[...]
    sent_d = over_visits(lambda step: d_ref, d_all, dsend, drecv)

    for load in loads[4:]:
        load.wait()
    cx = const_ref[:ORDER]
    cx_head, cx_tail = split(cx, 2)
    back = [dot(cx_head, res_ref[v], NT) + dot(cx_tail, res_ref[v], NT) for v in range(vis_local)]
    by_patch, by_row = [], []
    for v in range(vis_local):
        tw = tw_ref[v * ORDER : (v + 1) * ORDER]
        tw_high = tw.astype(BF16).astype(F32)
        tw = jnp.concatenate([tw_high, tw - tw_high], axis=0).astype(BF16)
        mixed = dot(jnp.concatenate([wscr[v], tw], axis=0), raw_ref[v], NN)
        by_patch.append(mixed[:npk])
        by_row.append(mixed[npk : npk + ORDER] + mixed[npk + ORDER :])
    design = d_ref[...]
    pa_ref[...] = wide_dot(jnp.concatenate(back, axis=1), jnp.concatenate(by_patch, axis=1), NT)
    sent_a = over_visits(lambda step: pa_ref, pa_recv, asend, arecv)

    lane_visit = iota((ORDER, LANES), 1) >> 3

    def own_blocks(full):
        total = jnp.zeros((ORDER, LANES), F32)
        for v in range(vis_local):
            total = total + jnp.where(lane_visit == v, full[v * ORDER : (v + 1) * ORDER], 0.0)
        return total

    def repeat(x):
        return jnp.concatenate([x] * (LANES // ORDER), axis=0)

    warped_moment = own_blocks(
        jnp.concatenate([wide_dot(by_row[v], repeat(back[v]), NT) for v in range(vis_local)], axis=0)
    )

    s_total = total_over_ccd(s_recv, ssend, srecv)
    s_ref[...] = s_total
    for q in range(2 * ORDER - 1):
        degree = abs(q - (ORDER - 1))
        sext_ref[q : q + 1] = s_ref[degree : degree + 1]
    lam = const_ref[2 * ORDER : 3 * ORDER, :LANES]
    sub = iota((ORDER, LANES), 0)
    system = []
    for b in range(ORDER):
        mean = 0.5 * (s_ref[b : b + ORDER] + sext_ref[ORDER - 1 - b : 2 * ORDER - 1 - b])
        system.append(lam * mean + jnp.where(sub == b, ridge_weight, 0.0))
    inverse = list(system)
    for k in range(ORDER):
        pivot = 1.0 / inverse[k][k : k + 1]
        off = jnp.where(sub == k, 0.0, inverse[k])
        for c in range(ORDER):
            if c != k:
                row = inverse[c][k : k + 1] * pivot
                inverse[c] = jnp.where(sub == k, row, inverse[c] - off * row)
        inverse[k] = jnp.where(sub == k, pivot, -off * pivot)

    def times(columns, x):
        total = columns[0] * x[0:1]
        for b in range(1, ORDER):
            total = total + columns[b] * x[b : b + 1]
        return total

    def solve(rhs):
        guess = times(inverse, rhs)
        return guess + times(inverse, rhs - times(system, guess))

    def spread(coefs):
        return [jnp.where(lane_visit == v, coefs, 0.0) for v in range(vis_local)]

    for copy in sent_d:
        copy.wait_recv()
    count = jnp.zeros((1, npk), F32)
    for step in range(n_v):
        for v in range(vis_local):
            count = count + d_all[step, v * ORDER : v * ORDER + 1]
    per_slot = 1.0 / (count + 1.0)
    design_all = d_all[...].reshape(n_v * nvb, npk)

    for copy in sent_a:
        copy.wait_recv()
    projected = pa_ref[...]
    for step in range(1, n_v):
        projected = projected + pa_recv[step]
    m_recv[ci] = warped_moment - own_blocks(wide_dot(design, repeat(projected * per_slot), NT))
    sent_b = over_ccd(m_recv, bsend, brecv)
    k_recv[ci] = wide_dot(design * per_slot, design_all, NT)
    sent_k = over_ccd(k_recv, ksend, krecv)
    mine = iota((P_DEV, npk), 1) == iota((P_DEV, npk), 0) + vi * P_DEV
    scale = jnp.where(mine, per_slot, 0.0)
    own_design = wide_dot(scale, design_all, NT)
    sums1 = jnp.zeros((npk, raw_ref.shape[2]), F32)
    for v in range(vis_local):
        high, low = split(by_patch[v], 2)
        sums1 = sums1 + (dot(high, res_ref[v], NN) + dot(low, res_ref[v], NN))
    s1_ref[...] = sums1

    def owner_rows(step):
        owner = lax.rem(vi + step, n_v)
        return s1_ref.at[pl.ds(pl.multiple_of(owner * P_DEV, P_DEV), P_DEV)]

    sent_g = over_visits(owner_rows, s1_recv, gsend, grecv)

    moment = total_over_ccd(m_recv, bsend, brecv)
    o_recv[0] = solve(moment)

    sent_c = over_visits(lambda step: o_recv.at[0], o_recv, csend, crecv)
    for copy in sent_g:
        copy.wait_recv()
    own = s1_ref[pl.ds(pl.multiple_of(vi * P_DEV, P_DEV), P_DEV)]
    for step in range(1, n_v):
        own = own + s1_recv[step]
    own = own * jnp.sum(scale, axis=1, keepdims=True)
    k_total = total_over_ccd(k_recv, ksend, krecv)
    for copy in sent_c:
        copy.wait_recv()
    coefs = []
    for step in range(n_v):
        coefs += spread(o_recv[step])
    fold = const_ref[ORDER : 2 * ORDER, :LANES]
    coefs = wide_dot(fold, jnp.concatenate(coefs, axis=0), NT)
    moment = moment + lam * own_blocks(wide_dot(k_total, repeat(coefs), NT))
    terms = wide_dot(jnp.concatenate(spread(solve(moment)), axis=0), const_ref[3 * ORDER :, :LANES], NT)
    own_b = (iota(terms.shape, 1) & (ORDER - 1)) == (iota(terms.shape, 0) & (ORDER - 1))
    terms = jnp.where(own_b, terms, 0.0)
    for v in range(vis_local):
        out_ref[P_DEV + v : P_DEV + v + 1, : ORDER * ORDER] = jnp.sum(
            terms[v * ORDER : (v + 1) * ORDER], axis=0, keepdims=True
        )
    out_ref[:P_DEV] = own - wide_dot(wide_dot(own_design, coefs, NT), cx, NN)

    for copy in sent_s + sent_d + sent_a + sent_g + sent_b + sent_k + sent_c:
        copy.wait_send()


def per_device(raw_rows, resample, slot_row, tap_weight, patch_id, live_mask):
    n_v, n_c = lax.axis_size("visit"), lax.axis_size("ccd")
    vis_local, rows, pixels = raw_rows.shape
    slots = slot_row.shape[3]
    npk, nvb = n_v * P_DEV, vis_local * ORDER
    consts = jnp.asarray(basis_constants(pixels, vis_local))
    vmem = pl.BlockSpec(memory_space=pltpu.VMEM)
    hbm = pl.BlockSpec(memory_space=pltpu.HBM)
    dma = pltpu.SemaphoreType.DMA
    packed = pl.pallas_call(
        functools.partial(kernel, n_v, n_c, vis_local),
        out_shape=pltpu.VMEM((P_DEV + 8 * (-(-vis_local // 8)), pixels), F32),
        in_specs=[hbm] * 7,
        out_specs=vmem,
        scratch_shapes=[
            pltpu.VMEM(slot_row.shape, jnp.int32),
            pltpu.VMEM(tap_weight.shape, F32),
            pltpu.VMEM(patch_id.shape, jnp.int32),
            pltpu.VMEM(live_mask.shape, jnp.int32),
            pltpu.VMEM(consts.shape, F32),
            pltpu.VMEM(raw_rows.shape, BF16),
            pltpu.VMEM(resample.shape, BF16),
            pltpu.VMEM((4, n_v, slots), jnp.int32),
            pltpu.VMEM((n_v, 2 * ORDER, slots), F32),
            pltpu.VMEM((vis_local, npk, rows), BF16),
            pltpu.VMEM((nvb, rows), F32),
            pltpu.VMEM((nvb, npk), F32),
            pltpu.VMEM((2 * ORDER, LANES), F32),
            pltpu.VMEM((2 * ORDER, LANES), F32),
            pltpu.VMEM((npk, pixels), F32),
            pltpu.VMEM((ORDER, npk), F32),
            pltpu.VMEM((n_v, nvb, npk), F32),
            pltpu.VMEM((n_c, 2 * ORDER, LANES), F32),
            pltpu.VMEM((n_c, ORDER, LANES), F32),
            pltpu.VMEM((n_c, nvb, n_v * nvb), F32),
            pltpu.VMEM((n_v, ORDER, npk), F32),
            pltpu.VMEM((n_v, ORDER, LANES), F32),
            pltpu.VMEM((n_v, P_DEV, pixels), F32),
            dma((7,)),
            dma((n_c,)), dma((n_c,)),
            dma((n_v,)), dma((n_v,)),
            dma((n_c,)), dma((n_c,)),
            dma((n_v,)), dma((n_v,)),
            dma((n_c,)), dma((n_c,)),
            dma((n_v,)), dma((n_v,)),
            dma((n_v,)), dma((n_v,)),
        ],
        compiler_params=pltpu.CompilerParams(
            collective_id=0, has_side_effects=True, vmem_limit_bytes=62 * 1024 * 1024
        ),
    )(slot_row, tap_weight, patch_id, live_mask, consts, raw_rows, resample)
    return (packed[P_DEV : P_DEV + vis_local, : ORDER * ORDER], packed[:P_DEV])


def solution(mesh):
    in_specs = (
        P("visit", "ccd", None),
        P("visit", None, None),
        P("visit", "ccd", None, None),
        P(None, "visit", "ccd", None, None),
        P("visit", "ccd", None, None),
        P("visit", "ccd", None, None),
    )
    out_specs = (P("visit", None), P(("visit", "ccd"), None))
    return jax.shard_map(
        per_device, mesh=mesh, in_specs=in_specs, out_specs=out_specs, check_vma=False
    )
```
